512 devices in a mesh: blk: 16 (over z), tp: 32 (over y, x, core).
Axes of the slice: x: 4, y: 4, z: 16, core: 2. Of those that a mesh axis runs over, the one named last changes fastest.
Arguments:
- weights: float32 [16, 28672, 384], P('blk', 'tp'), may hold values from -71 to 71
- hidden: bfloat16 [16384, 28672], P('blk', 'tp'), may hold values from -6 to 6
- grad_out: bfloat16 [16384, 384], P('blk'), may hold values from -6 to 6
- warm_start: float32 [16, 8, 384], replicated, may hold values from -6 to 6
Outputs:
- new_weights: float32 [16, 28672, 384], P('blk', 'tp')
- next_start: float32 [16, 8, 384], P('blk')
The draws below stay inside these ranges and needn't reach their ends.
All inputs are finite; a program needn't handle non-finite values.
Results may differ from the reference program's by a relative error of at most 0.0003.
Values sent between devices are 32-bit elements; how exact they have to be, the bound alone decides.
A program may use at most 64 MiB of HBM per device.

```python
import math
import jax
import jax.numpy as jnp
from jax import lax

FF = 28672
SLAB = 384
TOK_DEV = 1024
RANK = 8
TOKENS = 16384
N_BLK = 16


def draw_weights(key, part):
    key = jax.random.fold_in(key, 17)
    subkeys = jax.random.split(key, 3)
    single = jax.random.truncated_normal(subkeys[0], -4.0, 4.0, (N_BLK, FF, SLAB), jnp.float32)
    log_low = math.log(0.25)
    log_high = math.log(2.5)
    row_scale = jnp.exp(jax.random.uniform(subkeys[1], (N_BLK, FF, 1), jnp.float32, log_low, log_high))
    col_scale = jnp.exp(jax.random.uniform(subkeys[2], (N_BLK, 1, SLAB), jnp.float32, log_low, log_high))
    position = jnp.arange(FF, dtype=jnp.float32).reshape(1, FF, 1) / FF
    values = single
    trend_scale = jnp.exp(0.55 * position)
    return (values * row_scale * col_scale * trend_scale).astype(jnp.float32)


def shard_levels(rng, dims, shards, low, largest):
    factor_of = 1.0
    for dim, shards_of in shards:
        heights = jax.random.uniform(jax.random.fold_in(jax.random.fold_in(rng, 6), dim), (shards_of,), jnp.float32, low / len(shards), largest / len(shards))
        factor_of = factor_of * jnp.repeat(jnp.exp(heights), dims[dim] // shards_of).reshape((-1,) + (1,) * (len(dims) - 1 - dim))
    return factor_of


def noise(own_key, dims, width, bound, pieces=(), held_as=jnp.bfloat16):
    gain = shard_levels(own_key, dims, pieces, -0.22, 0.18) if pieces else 1.0
    array = jax.random.normal(own_key, dims, jnp.float32) * width * gain
    return jnp.minimum(jnp.maximum(array, -bound), bound).astype(held_as)


def setup_inputs(seed: int = 0) -> dict:
    key_of = jax.random.split(jax.random.key(seed), 5)
    weights = draw_weights(jax.random.fold_in(key_of[4], 71), 0)
    hidden = noise(key_of[1], (TOKENS, FF), 1.0, 6.0, ((0, 16), (1, 32)))
    grad_out = noise(key_of[2], (TOKENS, SLAB), 1.0, 6.0, ((0, 16),))
    warm_start = noise(key_of[3], (N_BLK, RANK, SLAB), 1.0, 6.0, (), jnp.float32)
    return {"weights": weights, "hidden": hidden, "grad_out": grad_out, "warm_start": warm_start}


step_rate = 0.5
mix_rate = 0.5

def forward_solve(lower_factor, rows):
    solved = []
    for column in range(lower_factor.shape[-1]):
        running = rows[..., column, :]
        for earlier in range(column):
            running = running - lower_factor[..., column, earlier][..., None] * solved[earlier]
        solved.append(running / lower_factor[..., column, column][..., None])
    return jnp.stack(solved, axis=-2)

def reference(weights, hidden, grad_out, warm_start):
    highest = lax.Precision.HIGHEST
    factor = step_rate / math.sqrt(TOK_DEV)
    hidden_blocks = hidden.reshape(N_BLK, TOK_DEV, FF)
    grad_blocks = grad_out.reshape(N_BLK, TOK_DEV, SLAB)

    def local_step(members):
        master, acts, cotangent = members
        gradient = jnp.dot(acts.T.astype(jnp.float32), cotangent.astype(jnp.float32), preferred_element_type=jnp.float32)
        return master - factor * gradient
    stepped = lax.map(local_step, (weights, hidden_blocks, grad_blocks))
    left_start = jnp.roll(warm_start, 1, axis=0)
    own_right = jnp.einsum('efs,ers->erf', stepped, warm_start, precision=highest)
    own_left = jnp.einsum('efs,ers->erf', stepped, left_start, precision=highest)
    images = own_right - jnp.roll(own_left, -1, axis=0)
    gram_matrix = jnp.einsum('erf,esf->ers', images, images, precision=highest)
    lower_factor = jnp.linalg.cholesky(gram_matrix)
    basis_rows = forward_solve(lower_factor, images)
    left_basis = jnp.roll(basis_rows, 1, axis=0)
    back_right = jnp.einsum('erf,efs->ers', basis_rows, stepped, precision=highest)
    back_left = jnp.einsum('erf,efs->ers', left_basis, stepped, precision=highest)
    next_start = back_right - jnp.roll(back_left, -1, axis=0)
    left_next = jnp.roll(next_start, 1, axis=0)

    def mixing(members):
        current, basis_here, next_here, basis_prior, next_prior = members
        correction = jnp.einsum('rf,rs->fs', basis_here, next_here, precision=highest)
        correction = correction - jnp.einsum('rf,rs->fs', basis_prior, next_prior, precision=highest)
        return current - mix_rate * correction
    new_weights = lax.map(mixing, (stepped, basis_rows, next_start, left_basis, left_next))
    return (new_weights, next_start)
```

```python
import functools
import math

import jax
import jax.numpy as jnp
from jax import lax
from jax.experimental import pallas as pl
from jax.experimental.pallas import tpu as pltpu
from jax.sharding import PartitionSpec as P

step_rate = 0.5
mix_rate = 0.5
MESH = pl.DeviceIdType.MESH
X, Y, C = 4, 4, 2
RANK = 8
PIECES = 14
F32, BF16 = jnp.float32, jnp.bfloat16


def split3(v):
    high = v.astype(BF16)
    rest = v - high.astype(F32)
    mid = rest.astype(BF16)
    low = (rest - mid.astype(F32)).astype(BF16)
    return high, mid, low


def dot(a, b, dims):
    return lax.dot_general(a, b, (dims, ((), ())), preferred_element_type=F32)


def six_pass(rows, stacks, dims):
    n = rows[0].shape[0]
    high, mid, low = stacks
    a = dot(jnp.concatenate(rows, axis=0), high, dims)
    b = dot(jnp.concatenate(rows[:2], axis=0), mid, dims)
    c = dot(rows[0], low, dims)
    small = a[2 * n :] + b[n:] + c
    return a[:n] + (a[n : 2 * n] + b[:n] + small)


def send(src, dst, send_sem, recv_sem, peer):
    copy = pltpu.make_async_remote_copy(
        src_ref=src, dst_ref=dst, send_sem=send_sem, recv_sem=recv_sem,
        device_id=peer, device_id_type=MESH,
    )
    copy.start()
    return copy


def kernel(
    count, chunks, factor,
    w_hbm, h_hbm, g_hbm, s_hbm, *rest,
):
    steps, images, rest = rest[:PIECES], rest[PIECES : 2 * PIECES], rest[2 * PIECES :]
    mix_ref, next_ref, w_v, h_v, g_v, start_v, parts_v, own, land, part = rest[:10]
    zbuf, zsum, xbuf, xsum, ybuf, load_sems = rest[10:16]
    isend, irecv, zsend, zrecv, xsend, xrecv, ysend, yrecv = rest[16:]
    tall_rows = steps[0].shape[0]
    r = lax.axis_index("blk")
    t = lax.axis_index("tp")
    core = lax.rem(t, C)
    x = lax.rem(lax.div(t, C), X)
    y = lax.div(t, C * X)
    right = lax.rem(r + 1, count)
    left = lax.rem(r + count - 1, count)
    chip = t - core
    slab = w_v.shape[1]

    def at(yy, xx, cc):
        return (yy * X + xx) * C + cc

    loads = [
        pltpu.make_async_copy(s_hbm.at[r], start_v.at[0], load_sems.at[1]),
        pltpu.make_async_copy(s_hbm.at[left], start_v.at[1], load_sems.at[2]),
        pltpu.make_async_copy(g_hbm, g_v, load_sems.at[0]),
    ]
    for copy in loads:
        copy.start()
    chunk_loads = []
    for i, (lo, size) in enumerate(chunks):
        w_copy = pltpu.make_async_copy(
            w_hbm.at[pl.ds(lo, size)], w_v.at[pl.ds(lo, size)], load_sems.at[4 + 2 * i]
        )
        h_copy = pltpu.make_async_copy(
            h_hbm.at[:, pl.ds(lo, size)], h_v.at[:, pl.ds(lo, size)], load_sems.at[3 + 2 * i]
        )
        w_copy.start()
        h_copy.start()
        chunk_loads.append((w_copy, h_copy))

    barrier = pltpu.get_barrier_semaphore()
    peers = [(right, chip), (right, chip + 1), (left, chip), (left, chip + 1), (r, chip + 1 - core)]
    for k in range(1, X):
        peers.append((r, at(y, lax.rem(x + k, X), core)))
    for k in range(1, Y):
        for cc in range(C):
            peers.append((r, at(lax.rem(y + k, Y), x, cc)))
    for peer in peers:
        pl.semaphore_signal(barrier, inc=1, device_id=peer, device_id_type=MESH)

    part[...] = jnp.zeros_like(part)
    for copy in loads:
        copy.wait()
    starts = start_v[...].reshape(2 * RANK, slab)
    start_parts = split3(starts)
    tall = jnp.concatenate(start_parts, axis=0)
    n = 2 * RANK
    felt = dot(tall, g_v[...], ((1,), (1,)))
    felt = factor * (felt[:n] + (felt[n : 2 * n] + felt[2 * n :]))
    felt_tall = jnp.concatenate(split3(felt), axis=0)

    image_copies = []
    for i, (lo, size) in enumerate(chunks):
        span = pl.ds(lo, size)
        chunk_loads[i][0].wait()
        image = six_pass(start_parts, split3(w_v[span, :]), ((1,), (1,)))
        chunk_loads[i][1].wait()
        pulled = dot(felt_tall, h_v[:, span], ((1,), (0,)))
        image = image - (pulled[:n] + (pulled[n : 2 * n] + pulled[2 * n :]))
        own[0, :, span] = image[:RANK]
        own[1, :, span] = image[RANK:]
        if i == 0:
            pl.semaphore_wait(barrier, len(peers))
        image_copies.append(
            (
                send(own.at[0, :, span], land.at[1, :, span], isend.at[2 * i], irecv.at[2 * i], (right, t)),
                send(own.at[1, :, span], land.at[0, :, span], isend.at[2 * i + 1], irecv.at[2 * i + 1], (left, t)),
            )
        )

    for lo, size in chunks:
        span = pl.ds(lo, size)
        gradient = dot(h_v[:, span], g_v[...], ((0,), (0,)))
        stepped = w_v[span, :] - factor * gradient
        for p in range(lo // tall_rows, (lo + size) // tall_rows):
            steps[p][...] = stepped[p * tall_rows - lo : (p + 1) * tall_rows - lo]
        stacks = split3(stepped)
        for k in range(3):
            parts_v[k, span, :] = stacks[k]

    product = jnp.zeros((n, slab), F32)
    gram = jnp.zeros((n, n), F32)
    saved = []
    for i, (lo, size) in enumerate(chunks):
        span = pl.ds(lo, size)
        for copy in image_copies[i]:
            copy.wait_recv()
        edge = [own[0, :, span] - land[0, :, span], land[1, :, span] - own[1, :, span]]
        pieces = split3(jnp.concatenate(edge, axis=0))
        product = product + six_pass(pieces, [parts_v[k, span, :] for k in range(3)], ((1,), (0,)))
        gram = gram + six_pass(pieces, pieces, ((1,), (1,)))
        saved.append(pieces)
    part[0, :, :slab] = product[:RANK]
    part[1, :, :slab] = -product[RANK:]
    part[0, :, slab : slab + RANK] = 0.5 * gram[:RANK, :RANK]
    part[1, :, slab : slab + RANK] = 0.5 * gram[RANK:, RANK:]

    z_copies = [
        send(part.at[0], zbuf.at[core], zsend.at[0], zrecv.at[core], (right, chip + 1)),
        send(part.at[1], zbuf.at[core], zsend.at[1], zrecv.at[core], (left, chip)),
        send(part.at[1 - core], zbuf.at[2], zsend.at[2], zrecv.at[2], (r, chip + 1 - core)),
    ]
    for i, (lo, size) in enumerate(chunks):
        high, mid, low = saved[i]
        stack = jnp.concatenate([high, high, high, mid, mid, low], axis=0)
        columns = stack.T
        for p in range(lo // tall_rows, (lo + size) // tall_rows):
            images[p][...] = columns[p * tall_rows - lo : (p + 1) * tall_rows - lo]

    def landed(buf, sem):
        pltpu.make_async_remote_copy(
            src_ref=buf, dst_ref=buf, send_sem=zsend.at[0], recv_sem=sem,
            device_id=(r, chip + 1 - core), device_id_type=MESH,
        ).wait_recv()

    for k in range(3):
        landed(zbuf.at[k], zrecv.at[k])
    zsum[...] = (part[core] + zbuf[2]) + (zbuf[0] + zbuf[1])

    x_copies = []
    for k in range(1, X):
        peer = lax.rem(x + k, X)
        x_copies.append(send(zsum, xbuf.at[x], xsend.at[k - 1], xrecv.at[x], (r, at(y, peer, core))))
    xbuf[x] = zsum[...]
    for k in range(1, X):
        slot = lax.rem(x + k, X)
        landed(xbuf.at[slot], xrecv.at[slot])
    xsum[...] = (xbuf[0] + xbuf[1]) + (xbuf[2] + xbuf[3])

    y_copies = []
    for k in range(1, Y):
        peer = lax.rem(y + k, Y)
        for cc in range(C):
            y_copies.append(
                send(
                    xsum, ybuf.at[core, y], ysend.at[1 + (k - 1) * C + cc], yrecv.at[core, y],
                    (r, at(peer, x, cc)),
                )
            )
    y_copies.append(
        send(xsum, ybuf.at[core, y], ysend.at[0], yrecv.at[core, y], (r, chip + 1 - core))
    )
    ybuf[core, y] = xsum[...]
    landed(ybuf.at[1 - core, y], yrecv.at[1 - core, y])
    for k in range(1, Y):
        slot = lax.rem(y + k, Y)
        for cc in range(C):
            landed(ybuf.at[cc, slot], yrecv.at[cc, slot])

    rows = lax.broadcasted_iota(jnp.int32, (RANK, 1), 0)
    work = [(ybuf[e, 0] + ybuf[e, 1]) + (ybuf[e, 2] + ybuf[e, 3]) for e in range(2)]
    ends = [[], []]
    for j in range(RANK):
        for e in range(2):
            a = work[e]
            column = a[:, slab + j : slab + j + 1]
            pivot = column[j : j + 1, :]
            row = a[j : j + 1, :]
            if e == 0:
                next_ref[j : j + 1, :] = row[:, :slab] / jnp.sqrt(pivot)
            work[e] = a - jnp.where(rows == j, 0.0, column / pivot) * row
            ends[e].append(pivot)
    kept = [work[e][:, :slab] / jnp.concatenate(ends[e], axis=0) for e in range(2)]
    mix_ref[:RANK] = mix_rate * kept[0]
    mix_ref[RANK:] = -mix_rate * kept[1]
    for pair in image_copies:
        for copy in pair:
            copy.wait_send()
    for copy in z_copies + x_copies + y_copies:
        copy.wait_send()


def finish(*refs):
    steps, images = refs[:PIECES], refs[PIECES : 2 * PIECES]
    mix_v, next_v, out_hbm, next_hbm, out_v, sems = refs[2 * PIECES :]
    tall = steps[0].shape[0]
    last = pltpu.make_async_copy(next_v, next_hbm, sems.at[PIECES])
    last.start()
    high, mid, low = split3(mix_v[...])
    mix_stack = jnp.concatenate([high, mid, low, high, mid, high], axis=0)
    stores = [last]
    for p in range(PIECES):
        span = pl.ds(p * tall, tall)
        out_v[span, :] = steps[p][...] - dot(images[p][...], mix_stack, ((1,), (0,)))
        store = pltpu.make_async_copy(out_v.at[span], out_hbm.at[span], sems.at[p])
        store.start()
        stores.append(store)
    for store in stores:
        store.wait()


def local(count, weights, hidden, grad_out, warm_start):
    _, rows, slab = weights.shape
    tokens = hidden.shape[0]
    factor = step_rate / math.sqrt(tokens)
    chunks = [(0, 512), (512, rows - 512)]
    n = len(chunks)
    wide = slab + 128
    terms = 12 * RANK
    in_vmem = pl.BlockSpec(memory_space=pltpu.VMEM)
    in_hbm = pl.BlockSpec(memory_space=pltpu.HBM)
    kept = pl.pallas_call(
        functools.partial(kernel, count, chunks, factor),
        out_shape=(
            *[jax.ShapeDtypeStruct((rows // PIECES, slab), F32)] * PIECES,
            *[jax.ShapeDtypeStruct((rows // PIECES, terms), BF16)] * PIECES,
            jax.ShapeDtypeStruct((2 * RANK, slab), F32),
            jax.ShapeDtypeStruct((RANK, slab), F32),
        ),
        in_specs=[in_hbm] * 4,
        out_specs=(in_vmem,) * (2 * PIECES + 2),
        scratch_shapes=[
            pltpu.VMEM((rows, slab), F32),
            pltpu.VMEM((tokens, rows), BF16),
            pltpu.VMEM((tokens, slab), BF16),
            pltpu.VMEM((2, RANK, slab), F32),
            pltpu.VMEM((3, rows, slab), BF16),
            pltpu.VMEM((2, RANK, rows), F32),
            pltpu.VMEM((2, RANK, rows), F32),
            pltpu.VMEM((2, RANK, wide), F32),
            pltpu.VMEM((3, RANK, wide), F32),
            pltpu.VMEM((RANK, wide), F32),
            pltpu.VMEM((X, RANK, wide), F32),
            pltpu.VMEM((RANK, wide), F32),
            pltpu.VMEM((C, Y, RANK, wide), F32),
            pltpu.SemaphoreType.DMA((3 + 2 * n,)),
            pltpu.SemaphoreType.DMA((2 * n,)),
            pltpu.SemaphoreType.DMA((2 * n,)),
            pltpu.SemaphoreType.DMA((3,)),
            pltpu.SemaphoreType.DMA((3,)),
            pltpu.SemaphoreType.DMA((X - 1,)),
            pltpu.SemaphoreType.DMA((X,)),
            pltpu.SemaphoreType.DMA((1 + (Y - 1) * C,)),
            pltpu.SemaphoreType.DMA((C, Y)),
        ],
        compiler_params=pltpu.CompilerParams(
            collective_id=0, has_side_effects=True, vmem_limit_bytes=53480 * 1024
        ),
    )(weights[0], hidden, grad_out, warm_start)
    new_weights, next_start = pl.pallas_call(
        finish,
        out_shape=(
            jax.ShapeDtypeStruct((rows, slab), F32),
            jax.ShapeDtypeStruct((RANK, slab), F32),
        ),
        in_specs=[in_vmem] * (2 * PIECES + 2),
        out_specs=(in_hbm,) * 2,
        scratch_shapes=[
            pltpu.VMEM((rows, slab), F32),
            pltpu.SemaphoreType.DMA((PIECES + 1,)),
        ],
        compiler_params=pltpu.CompilerParams(vmem_limit_bytes=53480 * 1024),
    )(*kept)
    return new_weights[None], next_start[None]


def solution(mesh):
    return jax.shard_map(
        functools.partial(local, mesh.shape["blk"]),
        mesh=mesh,
        in_specs=(P("blk", "tp", None), P("blk", "tp"), P("blk", None), P()),
        out_specs=(P("blk", "tp", None), P("blk", None, None)),
        check_vma=False,
    )
```

```python
import functools
import math

import jax
import jax.numpy as jnp
from jax import lax
from jax.experimental import pallas as pl
from jax.experimental.pallas import tpu as pltpu
from jax.sharding import PartitionSpec as P

step_rate = 0.5
mix_rate = 0.5
MESH = pl.DeviceIdType.MESH
X, Y, C = 4, 4, 2
RANK = 8
PIECES = 14
F32, BF16 = jnp.float32, jnp.bfloat16


def split3(v):
    high = v.astype(BF16)
    rest = v - high.astype(F32)
    mid = rest.astype(BF16)
    low = (rest - mid.astype(F32)).astype(BF16)
    return high, mid, low


def dot(a, b, dims):
    return lax.dot_general(a, b, (dims, ((), ())), preferred_element_type=F32)


def folded(v):
    n = v.shape[0] // 3
    return v[:n] + (v[n : 2 * n] + v[2 * n :])


def send(src, dst, send_sem, recv_sem, peer):
    copy = pltpu.make_async_remote_copy(
        src_ref=src, dst_ref=dst, send_sem=send_sem, recv_sem=recv_sem,
        device_id=peer, device_id_type=MESH,
    )
    copy.start()
    return copy


def kernel(
    count, chunks, factor,
    w_hbm, h_hbm, g_hbm, s_hbm, *rest,
):
    steps, images, rest = rest[:PIECES], rest[PIECES : 2 * PIECES], rest[2 * PIECES :]
    mix_ref, next_ref, w_v, h_v, g_v, start_v, parts_v, own, land, part = rest[:10]
    first, second, load_sems, isend, irecv, sends, recvs = rest[10:]
    tall_rows = steps[0].shape[0]
    r = lax.axis_index("blk")
    t = lax.axis_index("tp")
    core = lax.rem(t, C)
    x = lax.rem(lax.div(t, C), X)
    y = lax.div(t, C * X)
    right = lax.rem(r + 1, count)
    left = lax.rem(r + count - 1, count)
    chip = t - core
    slab = w_v.shape[1]

    def at(yy, xx, cc):
        return (yy * X + xx) * C + cc

    loads = [
        pltpu.make_async_copy(s_hbm.at[r], start_v.at[0], load_sems.at[1]),
        pltpu.make_async_copy(s_hbm.at[left], start_v.at[1], load_sems.at[2]),
        pltpu.make_async_copy(g_hbm, g_v, load_sems.at[0]),
    ]
    for copy in loads:
        copy.start()
    chunk_loads = []
    for i, (lo, size) in enumerate(chunks):
        w_copy = pltpu.make_async_copy(
            w_hbm.at[pl.ds(lo, size)], w_v.at[pl.ds(lo, size)], load_sems.at[4 + 2 * i]
        )
        h_copy = pltpu.make_async_copy(
            h_hbm.at[:, pl.ds(lo, size)], h_v.at[:, pl.ds(lo, size)], load_sems.at[3 + 2 * i]
        )
        w_copy.start()
        h_copy.start()
        chunk_loads.append((w_copy, h_copy))

    barrier = pltpu.get_barrier_semaphore()
    def turned(v, k, size):
        return lax.rem(v + k, size)

    peers = []
    for kx in range(X):
        for cc in range(C):
            for side in (left, right):
                peers.append((side, at(y, turned(x, kx, X), cc)))
    around = [(ky, kx, kc) for ky in range(Y) for kx in range(X) for kc in range(C)][1:]
    for ky, kx, kc in around:
        peers.append((r, at(turned(y, ky, Y), turned(x, kx, X), turned(core, kc, C))))
    for peer in peers:
        pl.semaphore_signal(barrier, inc=1, device_id=peer, device_id_type=MESH)

    part[...] = jnp.zeros_like(part)
    for copy in loads:
        copy.wait()
    starts = start_v[...].reshape(2 * RANK, slab)
    start_parts = split3(starts)
    tall = jnp.concatenate(start_parts, axis=0)
    n = 2 * RANK
    tall_t = tall.T
    grad_t = g_v[...].T
    felt = factor * folded(dot(tall, grad_t, ((1,), (0,))))
    felt_tall = jnp.concatenate(split3(felt), axis=0)

    image_copies = []
    for i, (lo, size) in enumerate(chunks):
        span = pl.ds(lo, size)
        chunk_loads[i][0].wait()
        high, mid, low = [dot(v, tall_t, ((1,), (0,))) for v in split3(w_v[span, :])]
        seen = (high + (mid + low)).T
        chunk_loads[i][1].wait()
        image = folded(seen - dot(felt_tall, h_v[:, span], ((1,), (0,))))
        own[0, :, span] = image[:RANK]
        own[1, :, span] = image[RANK:]
        if i == 0:
            pl.semaphore_wait(barrier, len(peers))
        image_copies.append(
            (
                send(own.at[0, :, span], land.at[1, :, span], isend.at[2 * i], irecv.at[2 * i], (right, t)),
                send(own.at[1, :, span], land.at[0, :, span], isend.at[2 * i + 1], irecv.at[2 * i + 1], (left, t)),
            )
        )

    for lo, size in chunks:
        span = pl.ds(lo, size)
        gradient = dot(grad_t, h_v[:, span], ((1,), (0,)))
        stepped = w_v[span, :] - factor * gradient.T
        for p in range(lo // tall_rows, (lo + size) // tall_rows):
            steps[p][...] = stepped[p * tall_rows - lo : (p + 1) * tall_rows - lo]
        stacks = split3(stepped)
        for k in range(3):
            parts_v[k, span, :] = stacks[k]

    product = jnp.zeros((3 * n, slab), F32)
    gram = jnp.zeros((3 * n, n), F32)
    saved = []
    for i, (lo, size) in enumerate(chunks):
        span = pl.ds(lo, size)
        for copy in image_copies[i]:
            copy.wait_recv()
        edge = [own[0, :, span] - land[0, :, span], land[1, :, span] - own[1, :, span]]
        pieces = split3(jnp.concatenate(edge, axis=0))
        rows = jnp.concatenate(pieces, axis=0)
        for k in range(3):
            product = product + dot(rows, parts_v[k, span, :], ((1,), (0,)))
            gram = gram + dot(rows, pieces[k], ((1,), (1,)))
        saved.append(pieces)
    product, gram = folded(product), folded(gram)
    for k in range(X - 1):
        part[0, k] = product[:RANK, 128 * k : 128 * (k + 1)]
        part[1, k] = -product[RANK:, 128 * k : 128 * (k + 1)]
    part[0, X - 1, :, :RANK] = 0.5 * gram[:RANK, :RANK]
    part[1, X - 1, :, :RANK] = 0.5 * gram[RANK:, RANK:]

    for kx in reversed(range(X)):
        tile = turned(x, kx, X)
        back = (-kx) % X
        slot = X * C + C * back + core
        send(part.at[0, tile], first.at[slot], sends.at[0], recvs.at[0], (right, at(y, tile, 1)))
        send(part.at[1, tile], first.at[slot], sends.at[0], recvs.at[0], (left, at(y, tile, 0)))
        for kc in range(C):
            if kx or kc:
                edge = turned(core, kc, C)
                send(part.at[edge, tile], first.at[C * back + kc], sends.at[0], recvs.at[0], (r, at(y, tile, edge)))
    first[0] = part[core, x]
    for i, (lo, size) in enumerate(chunks):
        high, mid, low = saved[i]
        stack = jnp.concatenate([high, high, high, mid, mid, low], axis=0)
        columns = stack.T
        for p in range(lo // tall_rows, (lo + size) // tall_rows):
            images[p][...] = columns[p * tall_rows - lo : (p + 1) * tall_rows - lo]

    def whole(buf, step):
        return pltpu.make_async_remote_copy(
            src_ref=buf, dst_ref=buf, send_sem=sends.at[step], recv_sem=recvs.at[step],
            device_id=(r, chip + 1 - core), device_id_type=MESH,
        )

    early = first.at[pl.ds(1, first.shape[0] - 1)]
    late = second.at[pl.ds(1, second.shape[0] - 1)]
    whole(early, 0).wait_recv()
    terms = [first[k] for k in range(first.shape[0])]
    while len(terms) > 1:
        terms = [a + b for a, b in zip(terms[::2], terms[1::2])]
    second[0] = terms[0]
    for ky, kx, kc in reversed(around):
        send(
            second.at[0], second.at[(((-ky) % Y) * X + (-kx) % X) * C + kc], sends.at[1], recvs.at[1],
            (r, at(turned(y, ky, Y), turned(x, kx, X), turned(core, kc, C))),
        )
    whole(late, 1).wait_recv()

    def total(e, tile):
        kx = lax.rem(tile - x + X, X)
        kc = lax.rem(e + core, C)
        own = [second[(lax.rem(k - y + Y, Y) * X + kx) * C + kc] for k in range(Y)]
        return (own[0] + own[1]) + (own[2] + own[3])

    place = lax.broadcasted_iota(jnp.int32, (RANK, 128), 0)
    gram = [total(e, X - 1) for e in range(2)]
    right_side = [[total(e, k) for k in range(X - 1)] for e in range(2)]
    columns = [[jnp.broadcast_to(a[:, j : j + 1], (RANK, 128)) for j in range(RANK)] for a in gram]

    def spread(v, j):
        return jnp.broadcast_to(v[j : j + 1, :], (RANK, 128))

    ends = [jnp.ones((RANK, 128), F32)] * 2
    for j in range(RANK):
        for e in range(2):
            pivot = spread(columns[e][j], j)
            scale = jnp.where(place == j, 0.0, columns[e][j] * (1.0 / pivot))
            if e == 0:
                root = 1.0 / jnp.sqrt(pivot[:1])
                for k, v in enumerate(right_side[e]):
                    next_ref[j : j + 1, 128 * k : 128 * (k + 1)] = v[j : j + 1, :] * root
            for k in range(j + 1, RANK):
                columns[e][k] = columns[e][k] - scale * spread(columns[e][k], j)
            right_side[e] = [v - scale * spread(v, j) for v in right_side[e]]
            ends[e] = jnp.where(place == j, pivot, ends[e])
    for e, sign in enumerate((mix_rate, -mix_rate)):
        inverse = sign / ends[e]
        for k, v in enumerate(right_side[e]):
            mix_ref[RANK * e : RANK * (e + 1), 128 * k : 128 * (k + 1)] = v * inverse
    for pair in image_copies:
        for copy in pair:
            copy.wait_send()
    whole(early, 0).wait_send()
    whole(late, 1).wait_send()


def finish(*refs):
    steps, images = refs[:PIECES], refs[PIECES : 2 * PIECES]
    mix_v, next_v, out_hbm, next_hbm, out_v, sems = refs[2 * PIECES :]
    tall = steps[0].shape[0]
    last = pltpu.make_async_copy(next_v, next_hbm, sems.at[PIECES])
    last.start()
    high, mid, low = split3(mix_v[...])
    mix_stack = jnp.concatenate([high, mid, low, high, mid, high], axis=0)
    stores = [last]
    for p in range(PIECES):
        span = pl.ds(p * tall, tall)
        out_v[span, :] = steps[p][...] - dot(images[p][...], mix_stack, ((1,), (0,)))
        store = pltpu.make_async_copy(out_v.at[span], out_hbm.at[span], sems.at[p])
        store.start()
        stores.append(store)
    for store in stores:
        store.wait()


def local(count, weights, hidden, grad_out, warm_start):
    _, rows, slab = weights.shape
    tokens = hidden.shape[0]
    factor = step_rate / math.sqrt(tokens)
    chunks = [(0, 512), (512, rows - 512)]
    n = len(chunks)
    terms = 12 * RANK
    in_vmem = pl.BlockSpec(memory_space=pltpu.VMEM)
    in_hbm = pl.BlockSpec(memory_space=pltpu.HBM)
    kept = pl.pallas_call(
        functools.partial(kernel, count, chunks, factor),
        out_shape=(
            *[jax.ShapeDtypeStruct((rows // PIECES, slab), F32)] * PIECES,
            *[jax.ShapeDtypeStruct((rows // PIECES, terms), BF16)] * PIECES,
            jax.ShapeDtypeStruct((2 * RANK, slab), F32),
            jax.ShapeDtypeStruct((RANK, slab), F32),
        ),
        in_specs=[in_hbm] * 4,
        out_specs=(in_vmem,) * (2 * PIECES + 2),
        scratch_shapes=[
            pltpu.VMEM((rows, slab), F32),
            pltpu.VMEM((tokens, rows), BF16),
            pltpu.VMEM((tokens, slab), BF16),
            pltpu.VMEM((2, RANK, slab), F32),
            pltpu.VMEM((3, rows, slab), BF16),
            pltpu.VMEM((2, RANK, rows), F32),
            pltpu.VMEM((2, RANK, rows), F32),
            pltpu.VMEM((2, X, RANK, 128), F32),
            pltpu.VMEM((2 * X * C, RANK, 128), F32),
            pltpu.VMEM((Y * X * C, RANK, 128), F32),
            pltpu.SemaphoreType.DMA((3 + 2 * n,)),
            pltpu.SemaphoreType.DMA((2 * n,)),
            pltpu.SemaphoreType.DMA((2 * n,)),
            pltpu.SemaphoreType.DMA((2,)),
            pltpu.SemaphoreType.DMA((2,)),
        ],
        compiler_params=pltpu.CompilerParams(
            collective_id=0, has_side_effects=True, vmem_limit_bytes=53480 * 1024
        ),
    )(weights[0], hidden, grad_out, warm_start)
    new_weights, next_start = pl.pallas_call(
        finish,
        out_shape=(
            jax.ShapeDtypeStruct((rows, slab), F32),
            jax.ShapeDtypeStruct((RANK, slab), F32),
        ),
        in_specs=[in_vmem] * (2 * PIECES + 2),
        out_specs=(in_hbm,) * 2,
        scratch_shapes=[
            pltpu.VMEM((rows, slab), F32),
            pltpu.SemaphoreType.DMA((PIECES + 1,)),
        ],
        compiler_params=pltpu.CompilerParams(vmem_limit_bytes=53480 * 1024),
    )(*kept)
    return new_weights[None], next_start[None]


def solution(mesh):
    return jax.shard_map(
        functools.partial(local, mesh.shape["blk"]),
        mesh=mesh,
        in_specs=(P("blk", "tp", None), P("blk", "tp"), P("blk", None), P()),
        out_specs=(P("blk", "tp", None), P("blk", None, None)),
        check_vma=False,
    )
```

```python
import functools
import math

import jax
import jax.numpy as jnp
from jax import lax
from jax.experimental import pallas as pl
from jax.experimental.pallas import tpu as pltpu
from jax.sharding import PartitionSpec as P

step_rate = 0.5
mix_rate = 0.5
MESH = pl.DeviceIdType.MESH
X, Y, C = 4, 4, 2
RANK = 8
PIECES = 14
F32, BF16 = jnp.float32, jnp.bfloat16


def split3(v):
    high = v.astype(BF16)
    rest = v - high.astype(F32)
    mid = rest.astype(BF16)
    low = (rest - mid.astype(F32)).astype(BF16)
    return high, mid, low


def dot(a, b, dims):
    return lax.dot_general(a, b, (dims, ((), ())), preferred_element_type=F32)


def folded(v):
    n = v.shape[0] // 3
    return v[:n] + (v[n : 2 * n] + v[2 * n :])


def send(src, dst, send_sem, recv_sem, peer):
    copy = pltpu.make_async_remote_copy(
        src_ref=src, dst_ref=dst, send_sem=send_sem, recv_sem=recv_sem,
        device_id=peer, device_id_type=MESH,
    )
    copy.start()
    return copy


def kernel(
    count, chunks, factor,
    w_hbm, h_hbm, g_hbm, s_hbm, *rest,
):
    steps, images, rest = rest[:PIECES], rest[PIECES : 2 * PIECES], rest[2 * PIECES :]
    mix_ref, next_ref, w_v, h_v, g_v, start_v, parts_v, own, land, part = rest[:10]
    first, second, load_sems, isend, irecv, sends, recvs = rest[10:]
    tall_rows = steps[0].shape[0]
    r = lax.axis_index("blk")
    t = lax.axis_index("tp")
    core = lax.rem(t, C)
    x = lax.rem(lax.div(t, C), X)
    y = lax.div(t, C * X)
    right = lax.rem(r + 1, count)
    left = lax.rem(r + count - 1, count)
    chip = t - core
    slab = w_v.shape[1]

    def at(yy, xx, cc):
        return (yy * X + xx) * C + cc

    loads = [
        pltpu.make_async_copy(s_hbm.at[r], start_v.at[0], load_sems.at[1]),
        pltpu.make_async_copy(s_hbm.at[left], start_v.at[1], load_sems.at[2]),
        pltpu.make_async_copy(g_hbm, g_v, load_sems.at[0]),
    ]
    for copy in loads:
        copy.start()
    chunk_loads = []
    for i, (lo, size) in enumerate(chunks):
        w_copy = pltpu.make_async_copy(
            w_hbm.at[pl.ds(lo, size)], w_v.at[pl.ds(lo, size)], load_sems.at[4 + 2 * i]
        )
        h_copy = pltpu.make_async_copy(
            h_hbm.at[:, pl.ds(lo, size)], h_v.at[:, pl.ds(lo, size)], load_sems.at[3 + 2 * i]
        )
        w_copy.start()
        chunk_loads.append((w_copy, h_copy))
    for pair in chunk_loads:
        pair[1].start()

    barrier = pltpu.get_barrier_semaphore()
    def turned(v, k, size):
        return lax.rem(v + k, size)

    peers = []
    for kx in range(X):
        for cc in range(C):
            for side in (left, right):
                peers.append((side, at(y, turned(x, kx, X), cc)))
    around = [(ky, kx, kc) for ky in range(Y) for kx in range(X) for kc in range(C)][1:]
    for ky, kx, kc in around:
        peers.append((r, at(turned(y, ky, Y), turned(x, kx, X), turned(core, kc, C))))
    for peer in peers:
        pl.semaphore_signal(barrier, inc=1, device_id=peer, device_id_type=MESH)

    part[...] = jnp.zeros_like(part)
    for copy in loads:
        copy.wait()
    starts = start_v[...].reshape(2 * RANK, slab)
    start_parts = split3(starts)
    tall = jnp.concatenate(start_parts, axis=0)
    n = 2 * RANK
    tall_t = tall.T
    grad_t = g_v[...].T
    felt = factor * folded(dot(tall, grad_t, ((1,), (0,))))
    felt_tall = jnp.concatenate(split3(felt), axis=0)

    seen = []
    for i, (lo, size) in enumerate(chunks):
        chunk_loads[i][0].wait()
        high, mid, low = [dot(v, tall_t, ((1,), (0,))) for v in split3(w_v[pl.ds(lo, size), :])]
        seen.append(folded((high + (mid + low)).T))
    image_copies = []
    for i, (lo, size) in enumerate(chunks):
        span = pl.ds(lo, size)
        chunk_loads[i][1].wait()
        image = seen[i] - folded(dot(felt_tall, h_v[:, span], ((1,), (0,))))
        own[0, :, span] = image[:RANK]
        own[1, :, span] = image[RANK:]
        if i == 0:
            pl.semaphore_wait(barrier, len(peers))
        image_copies.append(
            (
                send(own.at[0, :, span], land.at[1, :, span], isend.at[2 * i], irecv.at[2 * i], (right, t)),
                send(own.at[1, :, span], land.at[0, :, span], isend.at[2 * i + 1], irecv.at[2 * i + 1], (left, t)),
            )
        )

    for lo, size in chunks:
        span = pl.ds(lo, size)
        gradient = dot(grad_t, h_v[:, span], ((1,), (0,)))
        stepped = w_v[span, :] - factor * gradient.T
        for p in range(lo // tall_rows, (lo + size) // tall_rows):
            steps[p][...] = stepped[p * tall_rows - lo : (p + 1) * tall_rows - lo]
        stacks = split3(stepped)
        for k in range(3):
            parts_v[k, span, :] = stacks[k]

    images_f = [[], []]
    for e in range(2):
        product = jnp.zeros((3 * RANK, slab), F32)
        gram = jnp.zeros((3 * RANK, RANK), F32)
        for i, (lo, size) in enumerate(chunks):
            span = pl.ds(lo, size)
            image_copies[i][1 - e].wait_recv()
            image = own[0, :, span] - land[0, :, span] if e == 0 else land[1, :, span] - own[1, :, span]
            images_f[e].append(image)
            pieces = split3(image)
            rows = jnp.concatenate([v.astype(F32) for v in pieces], axis=0).astype(BF16)
            for k in range(3):
                product = product + dot(rows, parts_v[k, span, :], ((1,), (0,)))
                gram = gram + dot(rows, pieces[k], ((1,), (1,)))
        product, gram = folded(product), folded(gram)
        for k in range(X - 1):
            block = product[:, 128 * k : 128 * (k + 1)]
            part[e, k] = block if e == 0 else -block
        part[e, X - 1, :, :RANK] = 0.5 * gram
        aside = lax.rem(core + e, C)
        for kx in reversed(range(X)):
            tile = turned(x, kx, X)
            back = (-kx) % X
            side, taker = ((right, 1), (left, 0))[e]
            send(
                part.at[e, tile], first.at[X * C + C * back + core], sends.at[0], recvs.at[0],
                (side, at(y, tile, taker)),
            )

            def near():
                send(
                    part.at[e, tile], first.at[C * back + aside], sends.at[0], recvs.at[0],
                    (r, at(y, tile, e)),
                )

            if kx:
                near()
            else:
                pl.when(core != e)(near)
    first[0] = part[core, x]
    def whole(buf, step):
        return pltpu.make_async_remote_copy(
            src_ref=buf, dst_ref=buf, send_sem=sends.at[step], recv_sem=recvs.at[step],
            device_id=(r, chip + 1 - core), device_id_type=MESH,
        )

    early = first.at[pl.ds(1, first.shape[0] - 1)]
    late = second.at[pl.ds(1, second.shape[0] - 1)]
    whole(early, 0).wait_recv()
    terms = [first[k] for k in range(first.shape[0])]
    while len(terms) > 1:
        terms = [a + b for a, b in zip(terms[::2], terms[1::2])]
    second[0] = terms[0]
    for ky, kx, kc in reversed(around):
        send(
            second.at[0], second.at[(((-ky) % Y) * X + (-kx) % X) * C + kc], sends.at[1], recvs.at[1],
            (r, at(turned(y, ky, Y), turned(x, kx, X), turned(core, kc, C))),
        )
    for i, (lo, size) in enumerate(chunks):
        high, mid, low = split3(jnp.concatenate([images_f[0][i], images_f[1][i]], axis=0))
        stack = jnp.concatenate([high, high, high, mid, mid, low], axis=0)
        columns = stack.T
        for p in range(lo // tall_rows, (lo + size) // tall_rows):
            images[p][...] = columns[p * tall_rows - lo : (p + 1) * tall_rows - lo]
    whole(late, 1).wait_recv()

    def total(e, tile):
        kx = lax.rem(tile - x + X, X)
        kc = lax.rem(e + core, C)
        own = [second[(lax.rem(k - y + Y, Y) * X + kx) * C + kc] for k in range(Y)]
        return (own[0] + own[1]) + (own[2] + own[3])

    place = lax.broadcasted_iota(jnp.int32, (RANK, 128), 0)
    gram = [total(e, X - 1) for e in range(2)]
    right_side = [[total(e, k) for k in range(X - 1)] for e in range(2)]
    columns = [[jnp.broadcast_to(a[:, j : j + 1], (RANK, 128)) for j in range(RANK)] for a in gram]

    def spread(v, j):
        return jnp.broadcast_to(v[j : j + 1, :], (RANK, 128))

    ends = [jnp.ones((RANK, 128), F32)] * 2
    for j in range(RANK):
        for e in range(2):
            pivot = spread(columns[e][j], j)
            scale = jnp.where(place == j, 0.0, columns[e][j] * (1.0 / pivot))
            if e == 0:
                root = 1.0 / jnp.sqrt(pivot[:1])
                for k, v in enumerate(right_side[e]):
                    next_ref[j : j + 1, 128 * k : 128 * (k + 1)] = v[j : j + 1, :] * root
            for k in range(j + 1, RANK):
                columns[e][k] = columns[e][k] - scale * spread(columns[e][k], j)
            right_side[e] = [v - scale * spread(v, j) for v in right_side[e]]
            ends[e] = jnp.where(place == j, pivot, ends[e])
    for e, sign in enumerate((mix_rate, -mix_rate)):
        inverse = sign / ends[e]
        for k, v in enumerate(right_side[e]):
            mix_ref[RANK * e : RANK * (e + 1), 128 * k : 128 * (k + 1)] = v * inverse
    for pair in image_copies:
        for copy in pair:
            copy.wait_send()
    whole(early, 0).wait_send()
    whole(late, 1).wait_send()


def finish(*refs):
    steps, images = refs[:PIECES], refs[PIECES : 2 * PIECES]
    mix_v, next_v, out_hbm, next_hbm, out_v, sems = refs[2 * PIECES :]
    tall = steps[0].shape[0]
    last = pltpu.make_async_copy(next_v, next_hbm, sems.at[PIECES])
    last.start()
    high, mid, low = split3(mix_v[...])
    mix_stack = jnp.concatenate([high, mid, low, high, mid, high], axis=0)
    stores = [last]
    for p in range(PIECES):
        span = pl.ds(p * tall, tall)
        out_v[span, :] = steps[p][...] - dot(images[p][...], mix_stack, ((1,), (0,)))
        store = pltpu.make_async_copy(out_v.at[span], out_hbm.at[span], sems.at[p])
        store.start()
        stores.append(store)
    for store in stores:
        store.wait()


def local(count, weights, hidden, grad_out, warm_start):
    _, rows, slab = weights.shape
    tokens = hidden.shape[0]
    factor = step_rate / math.sqrt(tokens)
    chunks = [(0, 512), (512, rows - 512)]
    n = len(chunks)
    terms = 12 * RANK
    in_vmem = pl.BlockSpec(memory_space=pltpu.VMEM)
    in_hbm = pl.BlockSpec(memory_space=pltpu.HBM)
    kept = pl.pallas_call(
        functools.partial(kernel, count, chunks, factor),
        out_shape=(
            *[jax.ShapeDtypeStruct((rows // PIECES, slab), F32)] * PIECES,
            *[jax.ShapeDtypeStruct((rows // PIECES, terms), BF16)] * PIECES,
            jax.ShapeDtypeStruct((2 * RANK, slab), F32),
            jax.ShapeDtypeStruct((RANK, slab), F32),
        ),
        in_specs=[in_hbm] * 4,
        out_specs=(in_vmem,) * (2 * PIECES + 2),
        scratch_shapes=[
            pltpu.VMEM((rows, slab), F32),
            pltpu.VMEM((tokens, rows), BF16),
            pltpu.VMEM((tokens, slab), BF16),
            pltpu.VMEM((2, RANK, slab), F32),
            pltpu.VMEM((3, rows, slab), BF16),
            pltpu.VMEM((2, RANK, rows), F32),
            pltpu.VMEM((2, RANK, rows), F32),
            pltpu.VMEM((2, X, RANK, 128), F32),
            pltpu.VMEM((2 * X * C, RANK, 128), F32),
            pltpu.VMEM((Y * X * C, RANK, 128), F32),
            pltpu.SemaphoreType.DMA((3 + 2 * n,)),
            pltpu.SemaphoreType.DMA((2 * n,)),
            pltpu.SemaphoreType.DMA((2 * n,)),
            pltpu.SemaphoreType.DMA((2,)),
            pltpu.SemaphoreType.DMA((2,)),
        ],
        compiler_params=pltpu.CompilerParams(
            collective_id=0, has_side_effects=True, vmem_limit_bytes=53480 * 1024
        ),
    )(weights[0], hidden, grad_out, warm_start)
    new_weights, next_start = pl.pallas_call(
        finish,
        out_shape=(
            jax.ShapeDtypeStruct((rows, slab), F32),
            jax.ShapeDtypeStruct((RANK, slab), F32),
        ),
        in_specs=[in_vmem] * (2 * PIECES + 2),
        out_specs=(in_hbm,) * 2,
        scratch_shapes=[
            pltpu.VMEM((rows, slab), F32),
            pltpu.SemaphoreType.DMA((PIECES + 1,)),
        ],
        compiler_params=pltpu.CompilerParams(vmem_limit_bytes=53480 * 1024),
    )(*kept)
    return new_weights[None], next_start[None]


def solution(mesh):
    return jax.shard_map(
        functools.partial(local, mesh.shape["blk"]),
        mesh=mesh,
        in_specs=(P("blk", "tp", None), P("blk", "tp"), P("blk", None), P()),
        out_specs=(P("blk", "tp", None), P("blk", None, None)),
        check_vma=False,
    )
```

```python
import functools
import math

import jax
import jax.numpy as jnp
from jax import lax
from jax.experimental import pallas as pl
from jax.experimental.pallas import tpu as pltpu
from jax.sharding import PartitionSpec as P

step_rate = 0.5
mix_rate = 0.5
MESH = pl.DeviceIdType.MESH
X, Y, C = 4, 4, 2
RANK = 8
PIECES = 14
F32, BF16 = jnp.float32, jnp.bfloat16


def split3(v):
    high = v.astype(BF16)
    rest = v - high.astype(F32)
    mid = rest.astype(BF16)
    low = (rest - mid.astype(F32)).astype(BF16)
    return high, mid, low


def dot(a, b, dims):
    return lax.dot_general(a, b, (dims, ((), ())), preferred_element_type=F32)


def folded(v):
    n = v.shape[0] // 3
    return v[:n] + (v[n : 2 * n] + v[2 * n :])


def send(src, dst, send_sem, recv_sem, peer):
    copy = pltpu.make_async_remote_copy(
        src_ref=src, dst_ref=dst, send_sem=send_sem, recv_sem=recv_sem,
        device_id=peer, device_id_type=MESH,
    )
    copy.start()
    return copy


def kernel(
    count, chunks, factor,
    w_hbm, h_hbm, g_hbm, s_hbm, *rest,
):
    steps, images, rest = rest[:PIECES], rest[PIECES : 2 * PIECES], rest[2 * PIECES :]
    mix_ref, next_ref, w_v, h_v, g_v, start_v, parts_v, own, land, part = rest[:10]
    first, second, load_sems, isend, irecv, sends, recvs = rest[10:]
    tall_rows = steps[0].shape[0]
    r = lax.axis_index("blk")
    t = lax.axis_index("tp")
    core = lax.rem(t, C)
    x = lax.rem(lax.div(t, C), X)
    y = lax.div(t, C * X)
    right = lax.rem(r + 1, count)
    left = lax.rem(r + count - 1, count)
    chip = t - core
    slab = w_v.shape[1]

    def at(yy, xx, cc):
        return (yy * X + xx) * C + cc

    loads = [
        pltpu.make_async_copy(s_hbm.at[r], start_v.at[0], load_sems.at[1]),
        pltpu.make_async_copy(s_hbm.at[left], start_v.at[1], load_sems.at[2]),
        pltpu.make_async_copy(g_hbm, g_v, load_sems.at[0]),
    ]
    for copy in loads:
        copy.start()
    chunk_loads = []
    for i, (lo, size) in enumerate(chunks):
        w_copy = pltpu.make_async_copy(
            w_hbm.at[pl.ds(lo, size)], w_v.at[pl.ds(lo, size)], load_sems.at[4 + 2 * i]
        )
        h_copy = pltpu.make_async_copy(
            h_hbm.at[:, pl.ds(lo, size)], h_v.at[:, pl.ds(lo, size)], load_sems.at[3 + 2 * i]
        )
        w_copy.start()
        chunk_loads.append((w_copy, h_copy))
    for pair in chunk_loads:
        pair[1].start()

    barrier = pltpu.get_barrier_semaphore()
    def turned(v, k, size):
        return lax.rem(v + k, size)

    peers = []
    for kx in range(X):
        for cc in range(C):
            for side in (left, right):
                peers.append((side, at(y, turned(x, kx, X), cc)))
    around = [(ky, kx, kc) for ky in range(Y) for kx in range(X) for kc in range(C)][1:]
    around.sort(key=lambda k: -min(k[0], Y - k[0]) - min(k[1], X - k[1]))
    along_x = sorted(range(X), key=lambda k: -min(k, X - k))
    for ky, kx, kc in around:
        peers.append((r, at(turned(y, ky, Y), turned(x, kx, X), turned(core, kc, C))))

    def greet(some):
        for peer in some:
            pl.semaphore_signal(barrier, inc=1, device_id=peer, device_id_type=MESH)

    greet(peers[: 2 * X * C])

    part[...] = jnp.zeros_like(part)
    for copy in loads:
        copy.wait()
    starts = start_v[...].reshape(2 * RANK, slab)
    start_parts = split3(starts)
    tall = jnp.concatenate(start_parts, axis=0)
    n = 2 * RANK
    tall_t = tall.T
    grad_t = g_v[...].T
    felt = factor * folded(dot(tall, grad_t, ((1,), (0,))))
    felt_tall = jnp.concatenate(split3(felt), axis=0)
    greet(peers[2 * X * C :])

    seen = []
    for i, (lo, size) in enumerate(chunks):
        chunk_loads[i][0].wait()
        high, mid, low = [dot(v, tall_t, ((1,), (0,))) for v in split3(w_v[pl.ds(lo, size), :])]
        seen.append(folded((high + (mid + low)).T))
    image_copies = []
    for i, (lo, size) in enumerate(chunks):
        span = pl.ds(lo, size)
        chunk_loads[i][1].wait()
        image = seen[i] - folded(dot(felt_tall, h_v[:, span], ((1,), (0,))))
        own[0, :, span] = image[:RANK]
        own[1, :, span] = image[RANK:]
        if i == 0:
            pl.semaphore_wait(barrier, len(peers))
        image_copies.append(
            (
                send(own.at[0, :, span], land.at[1, :, span], isend.at[2 * i], irecv.at[2 * i], (right, t)),
                send(own.at[1, :, span], land.at[0, :, span], isend.at[2 * i + 1], irecv.at[2 * i + 1], (left, t)),
            )
        )

    for lo, size in chunks:
        span = pl.ds(lo, size)
        gradient = dot(grad_t, h_v[:, span], ((1,), (0,)))
        stepped = w_v[span, :] - factor * gradient.T
        for p in range(lo // tall_rows, (lo + size) // tall_rows):
            steps[p][...] = stepped[p * tall_rows - lo : (p + 1) * tall_rows - lo]
        stacks = split3(stepped)
        for k in range(3):
            parts_v[k, span, :] = stacks[k]

    images_f = [[], []]
    for e in range(2):
        product = jnp.zeros((3 * RANK, slab), F32)
        gram = jnp.zeros((3 * RANK, RANK), F32)
        for i, (lo, size) in enumerate(chunks):
            span = pl.ds(lo, size)
            image_copies[i][1 - e].wait_recv()
            image = own[0, :, span] - land[0, :, span] if e == 0 else land[1, :, span] - own[1, :, span]
            images_f[e].append(image)
            pieces = split3(image)
            rows = jnp.concatenate([v.astype(F32) for v in pieces], axis=0).astype(BF16)
            for k in range(3):
                product = product + dot(rows, parts_v[k, span, :], ((1,), (0,)))
                gram = gram + dot(rows, pieces[k], ((1,), (1,)))
        product, gram = folded(product), folded(gram)
        for k in range(X - 1):
            block = product[:, 128 * k : 128 * (k + 1)]
            part[e, k] = block if e == 0 else -block
        part[e, X - 1, :, :RANK] = 0.5 * gram
        aside = lax.rem(core + e, C)
        side, taker = ((right, 1), (left, 0))[e]
        for kx in along_x:
            tile = turned(x, kx, X)
            send(
                part.at[e, tile], first.at[X * C + C * ((-kx) % X) + core], sends.at[0], recvs.at[0],
                (side, at(y, tile, taker)),
            )
        for kx in along_x:
            tile = turned(x, kx, X)

            def near():
                send(
                    part.at[e, tile], first.at[C * ((-kx) % X) + aside], sends.at[0], recvs.at[0],
                    (r, at(y, tile, e)),
                )

            if kx:
                near()
            else:
                pl.when(core != e)(near)
    first[0] = part[core, x]
    def whole(buf, step):
        return pltpu.make_async_remote_copy(
            src_ref=buf, dst_ref=buf, send_sem=sends.at[step], recv_sem=recvs.at[step],
            device_id=(r, chip + 1 - core), device_id_type=MESH,
        )

    early = first.at[pl.ds(1, first.shape[0] - 1)]
    late = second.at[pl.ds(1, second.shape[0] - 1)]
    whole(early, 0).wait_recv()
    terms = [first[k] for k in range(first.shape[0])]
    while len(terms) > 1:
        terms = [a + b for a, b in zip(terms[::2], terms[1::2])]
    second[0] = terms[0]
    for ky, kx, kc in around:
        send(
            second.at[0], second.at[(((-ky) % Y) * X + (-kx) % X) * C + kc], sends.at[1], recvs.at[1],
            (r, at(turned(y, ky, Y), turned(x, kx, X), turned(core, kc, C))),
        )
    for i, (lo, size) in enumerate(chunks):
        high, mid, low = split3(jnp.concatenate([images_f[0][i], images_f[1][i]], axis=0))
        stack = jnp.concatenate([high, high, high, mid, mid, low], axis=0)
        columns = stack.T
        for p in range(lo // tall_rows, (lo + size) // tall_rows):
            images[p][...] = columns[p * tall_rows - lo : (p + 1) * tall_rows - lo]
    whole(late, 1).wait_recv()

    def total(e, tile):
        kx = lax.rem(tile - x + X, X)
        kc = lax.rem(e + core, C)
        own = [second[(lax.rem(k - y + Y, Y) * X + kx) * C + kc] for k in range(Y)]
        return (own[0] + own[1]) + (own[2] + own[3])

    place = lax.broadcasted_iota(jnp.int32, (RANK, 128), 0)
    gram = [total(e, X - 1) for e in range(2)]
    right_side = [[total(e, k) for k in range(X - 1)] for e in range(2)]
    columns = [[jnp.broadcast_to(a[:, j : j + 1], (RANK, 128)) for j in range(RANK)] for a in gram]

    def spread(v, j):
        return jnp.broadcast_to(v[j : j + 1, :], (RANK, 128))

    ends = [jnp.ones((RANK, 128), F32)] * 2
    for j in range(RANK):
        for e in range(2):
            pivot = spread(columns[e][j], j)
            scale = jnp.where(place == j, 0.0, columns[e][j] * (1.0 / pivot))
            if e == 0:
                root = 1.0 / jnp.sqrt(pivot[:1])
                for k, v in enumerate(right_side[e]):
                    next_ref[j : j + 1, 128 * k : 128 * (k + 1)] = v[j : j + 1, :] * root
            for k in range(j + 1, RANK):
                columns[e][k] = columns[e][k] - scale * spread(columns[e][k], j)
            right_side[e] = [v - scale * spread(v, j) for v in right_side[e]]
            ends[e] = jnp.where(place == j, pivot, ends[e])
    for e, sign in enumerate((mix_rate, -mix_rate)):
        inverse = sign / ends[e]
        for k, v in enumerate(right_side[e]):
            mix_ref[RANK * e : RANK * (e + 1), 128 * k : 128 * (k + 1)] = v * inverse
    for pair in image_copies:
        for copy in pair:
            copy.wait_send()
    whole(early, 0).wait_send()
    whole(late, 1).wait_send()


def finish(*refs):
    steps, images = refs[:PIECES], refs[PIECES : 2 * PIECES]
    mix_v, next_v, out_hbm, next_hbm, out_v, sems = refs[2 * PIECES :]
    tall = steps[0].shape[0]
    last = pltpu.make_async_copy(next_v, next_hbm, sems.at[PIECES])
    last.start()
    high, mid, low = split3(mix_v[...])
    mix_stack = jnp.concatenate([high, mid, low, high, mid, high], axis=0)
    stores = [last]
    for p in range(PIECES):
        span = pl.ds(p * tall, tall)
        out_v[span, :] = steps[p][...] - dot(images[p][...], mix_stack, ((1,), (0,)))
        store = pltpu.make_async_copy(out_v.at[span], out_hbm.at[span], sems.at[p])
        store.start()
        stores.append(store)
    for store in stores:
        store.wait()


def local(count, weights, hidden, grad_out, warm_start):
    _, rows, slab = weights.shape
    tokens = hidden.shape[0]
    factor = step_rate / math.sqrt(tokens)
    chunks = [(0, 512), (512, rows - 512)]
    n = len(chunks)
    terms = 12 * RANK
    in_vmem = pl.BlockSpec(memory_space=pltpu.VMEM)
    in_hbm = pl.BlockSpec(memory_space=pltpu.HBM)
    kept = pl.pallas_call(
        functools.partial(kernel, count, chunks, factor),
        out_shape=(
            *[jax.ShapeDtypeStruct((rows // PIECES, slab), F32)] * PIECES,
            *[jax.ShapeDtypeStruct((rows // PIECES, terms), BF16)] * PIECES,
            jax.ShapeDtypeStruct((2 * RANK, slab), F32),
            jax.ShapeDtypeStruct((RANK, slab), F32),
        ),
        in_specs=[in_hbm] * 4,
        out_specs=(in_vmem,) * (2 * PIECES + 2),
        scratch_shapes=[
            pltpu.VMEM((rows, slab), F32),
            pltpu.VMEM((tokens, rows), BF16),
            pltpu.VMEM((tokens, slab), BF16),
            pltpu.VMEM((2, RANK, slab), F32),
            pltpu.VMEM((3, rows, slab), BF16),
            pltpu.VMEM((2, RANK, rows), F32),
            pltpu.VMEM((2, RANK, rows), F32),
            pltpu.VMEM((2, X, RANK, 128), F32),
            pltpu.VMEM((2 * X * C, RANK, 128), F32),
            pltpu.VMEM((Y * X * C, RANK, 128), F32),
            pltpu.SemaphoreType.DMA((3 + 2 * n,)),
            pltpu.SemaphoreType.DMA((2 * n,)),
            pltpu.SemaphoreType.DMA((2 * n,)),
            pltpu.SemaphoreType.DMA((2,)),
            pltpu.SemaphoreType.DMA((2,)),
        ],
        compiler_params=pltpu.CompilerParams(
            collective_id=0, has_side_effects=True, vmem_limit_bytes=53480 * 1024
        ),
    )(weights[0], hidden, grad_out, warm_start)
    new_weights, next_start = pl.pallas_call(
        finish,
        out_shape=(
            jax.ShapeDtypeStruct((rows, slab), F32),
            jax.ShapeDtypeStruct((RANK, slab), F32),
        ),
        in_specs=[in_vmem] * (2 * PIECES + 2),
        out_specs=(in_hbm,) * 2,
        scratch_shapes=[
            pltpu.VMEM((rows, slab), F32),
            pltpu.SemaphoreType.DMA((PIECES + 1,)),
        ],
        compiler_params=pltpu.CompilerParams(vmem_limit_bytes=53480 * 1024),
    )(*kept)
    return new_weights[None], next_start[None]


def solution(mesh):
    return jax.shard_map(
        functools.partial(local, mesh.shape["blk"]),
        mesh=mesh,
        in_specs=(P("blk", "tp", None), P("blk", "tp"), P("blk", None), P()),
        out_specs=(P("blk", "tp", None), P("blk", None, None)),
        check_vma=False,
    )
```

```python
import functools
import math

import jax
import jax.numpy as jnp
from jax import lax
from jax.experimental import pallas as pl
from jax.experimental.pallas import tpu as pltpu
from jax.sharding import PartitionSpec as P

step_rate = 0.5
mix_rate = 0.5
MESH = pl.DeviceIdType.MESH
X, Y, C = 4, 4, 2
RANK = 8
PIECES = 14
F32, BF16 = jnp.float32, jnp.bfloat16


def split3(v):
    high = v.astype(BF16)
    rest = v - high.astype(F32)
    mid = rest.astype(BF16)
    low = (rest - mid.astype(F32)).astype(BF16)
    return high, mid, low


def dot(a, b, dims):
    return lax.dot_general(a, b, (dims, ((), ())), preferred_element_type=F32)


def folded(v):
    n = v.shape[0] // 3
    return v[:n] + (v[n : 2 * n] + v[2 * n :])


def send(src, dst, send_sem, recv_sem, peer):
    copy = pltpu.make_async_remote_copy(
        src_ref=src, dst_ref=dst, send_sem=send_sem, recv_sem=recv_sem,
        device_id=peer, device_id_type=MESH,
    )
    copy.start()
    return copy


def kernel(
    count, chunks, factor,
    w_hbm, h_hbm, g_hbm, s_hbm, *rest,
):
    steps, images, rest = rest[:PIECES], rest[PIECES : 2 * PIECES], rest[2 * PIECES :]
    mix_ref, next_ref, w_v, h_v, g_v, start_v, parts_v, own, land, part = rest[:10]
    first, second, load_sems, isend, irecv, sends, recvs, ready = rest[10:]
    tall_rows = steps[0].shape[0]
    r = lax.axis_index("blk")
    t = lax.axis_index("tp")
    core = lax.rem(t, C)
    x = lax.rem(lax.div(t, C), X)
    y = lax.div(t, C * X)
    right = lax.rem(r + 1, count)
    left = lax.rem(r + count - 1, count)
    chip = t - core
    slab = w_v.shape[1]

    def at(yy, xx, cc):
        return (yy * X + xx) * C + cc

    loads = [
        pltpu.make_async_copy(s_hbm.at[r], start_v.at[0], load_sems.at[1]),
        pltpu.make_async_copy(s_hbm.at[left], start_v.at[1], load_sems.at[2]),
        pltpu.make_async_copy(g_hbm, g_v, load_sems.at[0]),
    ]
    for copy in loads:
        copy.start()
    chunk_loads = []
    for i, (lo, size) in enumerate(chunks):
        w_copy = pltpu.make_async_copy(
            w_hbm.at[pl.ds(lo, size)], w_v.at[pl.ds(lo, size)], load_sems.at[4 + 2 * i]
        )
        h_copy = pltpu.make_async_copy(
            h_hbm.at[:, pl.ds(lo, size)], h_v.at[:, pl.ds(lo, size)], load_sems.at[3 + 2 * i]
        )
        w_copy.start()
        chunk_loads.append((w_copy, h_copy))
    for pair in chunk_loads:
        pair[1].start()

    barrier = pltpu.get_barrier_semaphore()
    def turned(v, k, size):
        return lax.rem(v + k, size)

    sibling = (r, chip + 1 - core)
    x_row = [(r, at(y, turned(x, k, X), core)) for k in range(1, X)]
    y_column = [(r, at(turned(y, k, Y), x, core)) for k in range(1, Y)]
    entry = [(right, t), (left, t), sibling] + x_row + y_column
    around = [(ky, kx, kc) for ky in range(Y) for kx in range(X) for kc in range(C)][1:]
    around.sort(key=lambda k: -min(k[0], Y - k[0]) - min(k[1], X - k[1]))
    along_x = sorted(range(X), key=lambda k: -min(k, X - k))

    def greet(some, sem):
        for peer in some:
            pl.semaphore_signal(sem, inc=1, device_id=peer, device_id_type=MESH)

    greet(entry, barrier)

    part[...] = jnp.zeros_like(part)
    for copy in loads:
        copy.wait()
    starts = start_v[...].reshape(2 * RANK, slab)
    start_parts = split3(starts)
    tall = jnp.concatenate(start_parts, axis=0)
    n = 2 * RANK
    tall_t = tall.T
    grad_t = g_v[...].T
    felt = factor * folded(dot(tall, grad_t, ((1,), (0,))))
    felt_tall = jnp.concatenate(split3(felt), axis=0)

    seen = []
    for i, (lo, size) in enumerate(chunks):
        chunk_loads[i][0].wait()
        high, mid, low = [dot(v, tall_t, ((1,), (0,))) for v in split3(w_v[pl.ds(lo, size), :])]
        seen.append(folded((high + (mid + low)).T))
    image_copies = []
    for i, (lo, size) in enumerate(chunks):
        span = pl.ds(lo, size)
        chunk_loads[i][1].wait()
        image = seen[i] - folded(dot(felt_tall, h_v[:, span], ((1,), (0,))))
        own[0, :, span] = image[:RANK]
        own[1, :, span] = image[RANK:]
        if i == 0:
            pl.semaphore_wait(barrier, len(entry))
            greet(x_row, ready.at[0])
        image_copies.append(
            (
                send(own.at[0, :, span], land.at[1, :, span], isend.at[2 * i], irecv.at[2 * i], (right, t)),
                send(own.at[1, :, span], land.at[0, :, span], isend.at[2 * i + 1], irecv.at[2 * i + 1], (left, t)),
            )
        )

    for lo, size in chunks:
        span = pl.ds(lo, size)
        gradient = dot(grad_t, h_v[:, span], ((1,), (0,)))
        stepped = w_v[span, :] - factor * gradient.T
        for p in range(lo // tall_rows, (lo + size) // tall_rows):
            steps[p][...] = stepped[p * tall_rows - lo : (p + 1) * tall_rows - lo]
        stacks = split3(stepped)
        for k in range(3):
            parts_v[k, span, :] = stacks[k]
        if lo == 0:
            pl.semaphore_wait(ready.at[0], len(x_row))
            greet([sibling], ready.at[1])
    pl.semaphore_wait(ready.at[1], 1)

    images_f = [[], []]
    for e in range(2):
        product = jnp.zeros((3 * RANK, slab), F32)
        gram = jnp.zeros((3 * RANK, RANK), F32)
        for i, (lo, size) in enumerate(chunks):
            span = pl.ds(lo, size)
            image_copies[i][1 - e].wait_recv()
            image = own[0, :, span] - land[0, :, span] if e == 0 else land[1, :, span] - own[1, :, span]
            images_f[e].append(image)
            pieces = split3(image)
            rows = jnp.concatenate([v.astype(F32) for v in pieces], axis=0).astype(BF16)
            for k in range(3):
                product = product + dot(rows, parts_v[k, span, :], ((1,), (0,)))
                gram = gram + dot(rows, pieces[k], ((1,), (1,)))
        product, gram = folded(product), folded(gram)
        for k in range(X - 1):
            block = product[:, 128 * k : 128 * (k + 1)]
            part[e, k] = block if e == 0 else -block
        part[e, X - 1, :, :RANK] = 0.5 * gram
        aside = lax.rem(core + e, C)
        side, taker = ((right, 1), (left, 0))[e]
        for kx in along_x:
            tile = turned(x, kx, X)
            send(
                part.at[e, tile], first.at[X * C + C * ((-kx) % X) + core], sends.at[0], recvs.at[0],
                (side, at(y, tile, taker)),
            )
        for kx in along_x:
            tile = turned(x, kx, X)

            def near():
                send(
                    part.at[e, tile], first.at[C * ((-kx) % X) + aside], sends.at[0], recvs.at[0],
                    (r, at(y, tile, e)),
                )

            if kx:
                near()
            else:
                pl.when(core != e)(near)
    first[0] = part[core, x]
    def whole(buf, step):
        return pltpu.make_async_remote_copy(
            src_ref=buf, dst_ref=buf, send_sem=sends.at[step], recv_sem=recvs.at[step],
            device_id=(r, chip + 1 - core), device_id_type=MESH,
        )

    early = first.at[pl.ds(1, first.shape[0] - 1)]
    late = second.at[pl.ds(1, second.shape[0] - 1)]
    whole(early, 0).wait_recv()
    terms = [first[k] for k in range(first.shape[0])]
    while len(terms) > 1:
        terms = [a + b for a, b in zip(terms[::2], terms[1::2])]
    second[0] = terms[0]
    for ky, kx, kc in around:
        send(
            second.at[0], second.at[(((-ky) % Y) * X + (-kx) % X) * C + kc], sends.at[1], recvs.at[1],
            (r, at(turned(y, ky, Y), turned(x, kx, X), turned(core, kc, C))),
        )
    for i, (lo, size) in enumerate(chunks):
        high, mid, low = split3(jnp.concatenate([images_f[0][i], images_f[1][i]], axis=0))
        stack = jnp.concatenate([high, high, high, mid, mid, low], axis=0)
        columns = stack.T
        for p in range(lo // tall_rows, (lo + size) // tall_rows):
            images[p][...] = columns[p * tall_rows - lo : (p + 1) * tall_rows - lo]
    whole(late, 1).wait_recv()

    def total(e, tile):
        kx = lax.rem(tile - x + X, X)
        kc = lax.rem(e + core, C)
        own = [second[(lax.rem(k - y + Y, Y) * X + kx) * C + kc] for k in range(Y)]
        return (own[0] + own[1]) + (own[2] + own[3])

    place = lax.broadcasted_iota(jnp.int32, (RANK, 128), 0)
    gram = [total(e, X - 1) for e in range(2)]
    right_side = [[total(e, k) for k in range(X - 1)] for e in range(2)]
    columns = [[jnp.broadcast_to(a[:, j : j + 1], (RANK, 128)) for j in range(RANK)] for a in gram]

    def spread(v, j):
        return jnp.broadcast_to(v[j : j + 1, :], (RANK, 128))

    ends = [jnp.ones((RANK, 128), F32)] * 2
    for j in range(RANK):
        for e in range(2):
            pivot = spread(columns[e][j], j)
            scale = jnp.where(place == j, 0.0, columns[e][j] * (1.0 / pivot))
            if e == 0:
                root = 1.0 / jnp.sqrt(pivot[:1])
                for k, v in enumerate(right_side[e]):
                    next_ref[j : j + 1, 128 * k : 128 * (k + 1)] = v[j : j + 1, :] * root
            for k in range(j + 1, RANK):
                columns[e][k] = columns[e][k] - scale * spread(columns[e][k], j)
            right_side[e] = [v - scale * spread(v, j) for v in right_side[e]]
            ends[e] = jnp.where(place == j, pivot, ends[e])
    for e, sign in enumerate((mix_rate, -mix_rate)):
        inverse = sign / ends[e]
        for k, v in enumerate(right_side[e]):
            mix_ref[RANK * e : RANK * (e + 1), 128 * k : 128 * (k + 1)] = v * inverse
    for pair in image_copies:
        for copy in pair:
            copy.wait_send()
    whole(early, 0).wait_send()
    whole(late, 1).wait_send()


def finish(*refs):
    steps, images = refs[:PIECES], refs[PIECES : 2 * PIECES]
    mix_v, next_v, out_hbm, next_hbm, out_v, sems = refs[2 * PIECES :]
    tall = steps[0].shape[0]
    last = pltpu.make_async_copy(next_v, next_hbm, sems.at[PIECES])
    last.start()
    high, mid, low = split3(mix_v[...])
    mix_stack = jnp.concatenate([high, mid, low, high, mid, high], axis=0)
    stores = [last]
    for p in range(PIECES):
        span = pl.ds(p * tall, tall)
        out_v[span, :] = steps[p][...] - dot(images[p][...], mix_stack, ((1,), (0,)))
        store = pltpu.make_async_copy(out_v.at[span], out_hbm.at[span], sems.at[p])
        store.start()
        stores.append(store)
    for store in stores:
        store.wait()


def local(count, weights, hidden, grad_out, warm_start):
    _, rows, slab = weights.shape
    tokens = hidden.shape[0]
    factor = step_rate / math.sqrt(tokens)
    chunks = [(0, 512), (512, rows - 512)]
    n = len(chunks)
    terms = 12 * RANK
    in_vmem = pl.BlockSpec(memory_space=pltpu.VMEM)
    in_hbm = pl.BlockSpec(memory_space=pltpu.HBM)
    kept = pl.pallas_call(
        functools.partial(kernel, count, chunks, factor),
        out_shape=(
            *[jax.ShapeDtypeStruct((rows // PIECES, slab), F32)] * PIECES,
            *[jax.ShapeDtypeStruct((rows // PIECES, terms), BF16)] * PIECES,
            jax.ShapeDtypeStruct((2 * RANK, slab), F32),
            jax.ShapeDtypeStruct((RANK, slab), F32),
        ),
        in_specs=[in_hbm] * 4,
        out_specs=(in_vmem,) * (2 * PIECES + 2),
        scratch_shapes=[
            pltpu.VMEM((rows, slab), F32),
            pltpu.VMEM((tokens, rows), BF16),
            pltpu.VMEM((tokens, slab), BF16),
            pltpu.VMEM((2, RANK, slab), F32),
            pltpu.VMEM((3, rows, slab), BF16),
            pltpu.VMEM((2, RANK, rows), F32),
            pltpu.VMEM((2, RANK, rows), F32),
            pltpu.VMEM((2, X, RANK, 128), F32),
            pltpu.VMEM((2 * X * C, RANK, 128), F32),
            pltpu.VMEM((Y * X * C, RANK, 128), F32),
            pltpu.SemaphoreType.DMA((3 + 2 * n,)),
            pltpu.SemaphoreType.DMA((2 * n,)),
            pltpu.SemaphoreType.DMA((2 * n,)),
            pltpu.SemaphoreType.DMA((2,)),
            pltpu.SemaphoreType.DMA((2,)),
            pltpu.SemaphoreType.REGULAR((2,)),
        ],
        compiler_params=pltpu.CompilerParams(
            collective_id=0, has_side_effects=True, vmem_limit_bytes=53480 * 1024
        ),
    )(weights[0], hidden, grad_out, warm_start)
    new_weights, next_start = pl.pallas_call(
        finish,
        out_shape=(
            jax.ShapeDtypeStruct((rows, slab), F32),
            jax.ShapeDtypeStruct((RANK, slab), F32),
        ),
        in_specs=[in_vmem] * (2 * PIECES + 2),
        out_specs=(in_hbm,) * 2,
        scratch_shapes=[
            pltpu.VMEM((rows, slab), F32),
            pltpu.SemaphoreType.DMA((PIECES + 1,)),
        ],
        compiler_params=pltpu.CompilerParams(vmem_limit_bytes=53480 * 1024),
    )(*kept)
    return new_weights[None], next_start[None]


def solution(mesh):
    return jax.shard_map(
        functools.partial(local, mesh.shape["blk"]),
        mesh=mesh,
        in_specs=(P("blk", "tp", None), P("blk", "tp"), P("blk", None), P()),
        out_specs=(P("blk", "tp", None), P("blk", None, None)),
        check_vma=False,
    )
```

```python
import functools
import math

import jax
import jax.numpy as jnp
from jax import lax
from jax.experimental import pallas as pl
from jax.experimental.pallas import tpu as pltpu
from jax.sharding import PartitionSpec as P

step_rate = 0.5
mix_rate = 0.5
MESH = pl.DeviceIdType.MESH
X, Y, C = 4, 4, 2
RANK = 8
PIECES = 14
F32, BF16 = jnp.float32, jnp.bfloat16


def split3(v):
    high = v.astype(BF16)
    rest = v - high.astype(F32)
    mid = rest.astype(BF16)
    low = (rest - mid.astype(F32)).astype(BF16)
    return high, mid, low


def dot(a, b, dims):
    return lax.dot_general(a, b, (dims, ((), ())), preferred_element_type=F32)


def folded(v):
    n = v.shape[0] // 3
    return v[:n] + (v[n : 2 * n] + v[2 * n :])


def send(src, dst, send_sem, recv_sem, peer):
    copy = pltpu.make_async_remote_copy(
        src_ref=src, dst_ref=dst, send_sem=send_sem, recv_sem=recv_sem,
        device_id=peer, device_id_type=MESH,
    )
    copy.start()
    return copy


def kernel(
    count, chunks, factor,
    w_hbm, h_hbm, g_hbm, s_hbm, *rest,
):
    steps, images, rest = rest[:PIECES], rest[PIECES : 2 * PIECES], rest[2 * PIECES :]
    mix_ref, next_ref, w_v, h_v, g_v, start_v, parts_v, own, land, part = rest[:10]
    first, second, load_sems, isend, irecv, sends, recvs, ready = rest[10:]
    tall_rows = steps[0].shape[0]
    r = lax.axis_index("blk")
    t = lax.axis_index("tp")
    core = lax.rem(t, C)
    x = lax.rem(lax.div(t, C), X)
    y = lax.div(t, C * X)
    right = lax.rem(r + 1, count)
    left = lax.rem(r + count - 1, count)
    chip = t - core
    slab = w_v.shape[1]

    def at(yy, xx, cc):
        return (yy * X + xx) * C + cc

    loads = [
        pltpu.make_async_copy(s_hbm.at[r], start_v.at[0], load_sems.at[1]),
        pltpu.make_async_copy(s_hbm.at[left], start_v.at[1], load_sems.at[2]),
        pltpu.make_async_copy(g_hbm, g_v, load_sems.at[0]),
    ]
    for copy in loads:
        copy.start()
    chunk_loads = []
    for i, (lo, size) in enumerate(chunks):
        w_copy = pltpu.make_async_copy(
            w_hbm.at[pl.ds(lo, size)], w_v.at[pl.ds(lo, size)], load_sems.at[4 + 2 * i]
        )
        h_copy = pltpu.make_async_copy(
            h_hbm.at[:, pl.ds(lo, size)], h_v.at[:, pl.ds(lo, size)], load_sems.at[3 + 2 * i]
        )
        w_copy.start()
        chunk_loads.append((w_copy, h_copy))
    for pair in chunk_loads:
        pair[1].start()

    barrier = pltpu.get_barrier_semaphore()
    def turned(v, k, size):
        return lax.rem(v + k, size)

    sibling = (r, chip + 1 - core)
    x_row = [(r, at(y, turned(x, k, X), core)) for k in range(1, X)]
    y_column = [(r, at(turned(y, k, Y), x, core)) for k in range(1, Y)]
    entry = [(side, chip + cc) for side in (right, left) for cc in range(C)] + [sibling] + x_row + y_column
    around = [(ky, kx, kc) for ky in range(Y) for kx in range(X) for kc in range(C)][1:]
    around.sort(key=lambda k: -min(k[0], Y - k[0]) - min(k[1], X - k[1]))
    along_x = sorted(range(X), key=lambda k: -min(k, X - k))

    def greet(some, sem):
        for peer in some:
            pl.semaphore_signal(sem, inc=1, device_id=peer, device_id_type=MESH)

    greet(entry, barrier)

    part[...] = jnp.zeros_like(part)
    for copy in loads:
        copy.wait()
    starts = start_v[...].reshape(2 * RANK, slab)
    start_parts = split3(starts)
    tall = jnp.concatenate(start_parts, axis=0)
    n = 2 * RANK
    tall_t = tall.T
    grad_t = g_v[...].T
    felt = factor * folded(dot(tall, grad_t, ((1,), (0,))))
    felt_tall = jnp.concatenate(split3(felt), axis=0)

    seen = []
    for i, (lo, size) in enumerate(chunks):
        chunk_loads[i][0].wait()
        high, mid, low = [dot(v, tall_t, ((1,), (0,))) for v in split3(w_v[pl.ds(lo, size), :])]
        seen.append(folded((high + (mid + low)).T))
    image_copies = []
    for i, (lo, size) in enumerate(chunks):
        span = pl.ds(lo, size)
        chunk_loads[i][1].wait()
        image = seen[i] - folded(dot(felt_tall, h_v[:, span], ((1,), (0,))))
        own[0, :, span] = image[:RANK]
        own[1, :, span] = image[RANK:]
        if i == 0:
            pl.semaphore_wait(barrier, len(entry))
            greet(x_row, ready.at[0])
        image_copies.append(
            (
                send(own.at[0, :, span], land.at[1, :, span], isend.at[2 * i], irecv.at[2 * i], (right, t)),
                send(own.at[1, :, span], land.at[0, :, span], isend.at[2 * i + 1], irecv.at[2 * i + 1], (left, t)),
            )
        )

    for lo, size in chunks:
        span = pl.ds(lo, size)
        gradient = dot(grad_t, h_v[:, span], ((1,), (0,)))
        stepped = w_v[span, :] - factor * gradient.T
        for p in range(lo // tall_rows, (lo + size) // tall_rows):
            steps[p][...] = stepped[p * tall_rows - lo : (p + 1) * tall_rows - lo]
        stacks = split3(stepped)
        for k in range(3):
            parts_v[k, span, :] = stacks[k]

    images_f = [[], []]
    for e in range(2):
        product = jnp.zeros((3 * RANK, slab), F32)
        gram = jnp.zeros((3 * RANK, RANK), F32)
        for i, (lo, size) in enumerate(chunks):
            span = pl.ds(lo, size)
            image_copies[i][1 - e].wait_recv()
            image = own[0, :, span] - land[0, :, span] if e == 0 else land[1, :, span] - own[1, :, span]
            images_f[e].append(image)
            pieces = split3(image)
            rows = jnp.concatenate([v.astype(F32) for v in pieces], axis=0).astype(BF16)
            for k in range(3):
                product = product + dot(rows, parts_v[k, span, :], ((1,), (0,)))
                gram = gram + dot(rows, pieces[k], ((1,), (1,)))
        product, gram = folded(product), folded(gram)
        for k in range(X - 1):
            block = product[:, 128 * k : 128 * (k + 1)]
            part[e, k] = block if e == 0 else -block
        part[e, X - 1, :, :RANK] = 0.5 * gram
        aside = lax.rem(core + e, C)
        side, taker = ((right, 1), (left, 0))[e]
        if e == 0:
            pl.semaphore_wait(ready.at[0], len(x_row))
            greet([sibling], ready.at[1])

        def across():
            for kx in along_x:
                tile = turned(x, kx, X)
                send(
                    part.at[e, tile], first.at[X * C + C * ((-kx) % X) + core], sends.at[0], recvs.at[0],
                    (side, at(y, tile, taker)),
                )

        def within():
            for kx in along_x:
                tile = turned(x, kx, X)

                def near():
                    send(
                        part.at[e, tile], first.at[C * ((-kx) % X) + aside], sends.at[0], recvs.at[0],
                        (r, at(y, tile, e)),
                    )

                if kx:
                    near()
                else:
                    pl.when(core != e)(near)

        for step in (across, within) if e == 0 else (within, across):
            step()
    first[0] = part[core, x]
    def whole(buf, step):
        return pltpu.make_async_remote_copy(
            src_ref=buf, dst_ref=buf, send_sem=sends.at[step], recv_sem=recvs.at[step],
            device_id=(r, chip + 1 - core), device_id_type=MESH,
        )

    early = first.at[pl.ds(1, first.shape[0] - 1)]
    late = second.at[pl.ds(1, second.shape[0] - 1)]
    whole(early, 0).wait_recv()
    terms = [first[k] for k in range(first.shape[0])]
    while len(terms) > 1:
        terms = [a + b for a, b in zip(terms[::2], terms[1::2])]
    second[0] = terms[0]
    pl.semaphore_wait(ready.at[1], 1)
    for ky, kx, kc in around:
        send(
            second.at[0], second.at[(((-ky) % Y) * X + (-kx) % X) * C + kc], sends.at[1], recvs.at[1],
            (r, at(turned(y, ky, Y), turned(x, kx, X), turned(core, kc, C))),
        )
    for i, (lo, size) in enumerate(chunks):
        high, mid, low = split3(jnp.concatenate([images_f[0][i], images_f[1][i]], axis=0))
        stack = jnp.concatenate([high, high, high, mid, mid, low], axis=0)
        columns = stack.T
        for p in range(lo // tall_rows, (lo + size) // tall_rows):
            images[p][...] = columns[p * tall_rows - lo : (p + 1) * tall_rows - lo]
    whole(late, 1).wait_recv()

    def total(e, tile):
        kx = lax.rem(tile - x + X, X)
        kc = lax.rem(e + core, C)
        own = [second[(lax.rem(k - y + Y, Y) * X + kx) * C + kc] for k in range(Y)]
        return (own[0] + own[1]) + (own[2] + own[3])

    place = lax.broadcasted_iota(jnp.int32, (RANK, 128), 0)
    gram = [total(e, X - 1) for e in range(2)]
    right_side = [[total(e, k) for k in range(X - 1)] for e in range(2)]
    columns = [[jnp.broadcast_to(a[:, j : j + 1], (RANK, 128)) for j in range(RANK)] for a in gram]

    def spread(v, j):
        return jnp.broadcast_to(v[j : j + 1, :], (RANK, 128))

    ends = [jnp.ones((RANK, 128), F32)] * 2
    for j in range(RANK):
        for e in range(2):
            pivot = spread(columns[e][j], j)
            scale = jnp.where(place == j, 0.0, columns[e][j] * (1.0 / pivot))
            if e == 0:
                root = 1.0 / jnp.sqrt(pivot[:1])
                for k, v in enumerate(right_side[e]):
                    next_ref[j : j + 1, 128 * k : 128 * (k + 1)] = v[j : j + 1, :] * root
            for k in range(j + 1, RANK):
                columns[e][k] = columns[e][k] - scale * spread(columns[e][k], j)
            right_side[e] = [v - scale * spread(v, j) for v in right_side[e]]
            ends[e] = jnp.where(place == j, pivot, ends[e])
    for e, sign in enumerate((mix_rate, -mix_rate)):
        inverse = sign / ends[e]
        for k, v in enumerate(right_side[e]):
            mix_ref[RANK * e : RANK * (e + 1), 128 * k : 128 * (k + 1)] = v * inverse
    for pair in image_copies:
        for copy in pair:
            copy.wait_send()
    whole(early, 0).wait_send()
    whole(late, 1).wait_send()


def finish(*refs):
    steps, images = refs[:PIECES], refs[PIECES : 2 * PIECES]
    mix_v, next_v, out_hbm, next_hbm, out_v, sems = refs[2 * PIECES :]
    tall = steps[0].shape[0]
    last = pltpu.make_async_copy(next_v, next_hbm, sems.at[PIECES])
    last.start()
    high, mid, low = split3(mix_v[...])
    mix_stack = jnp.concatenate([high, mid, low, high, mid, high], axis=0)
    stores = [last]
    for p in range(PIECES):
        span = pl.ds(p * tall, tall)
        out_v[span, :] = steps[p][...] - dot(images[p][...], mix_stack, ((1,), (0,)))
        store = pltpu.make_async_copy(out_v.at[span], out_hbm.at[span], sems.at[p])
        store.start()
        stores.append(store)
    for store in stores:
        store.wait()


def local(count, weights, hidden, grad_out, warm_start):
    _, rows, slab = weights.shape
    tokens = hidden.shape[0]
    factor = step_rate / math.sqrt(tokens)
    chunks = [(0, 512), (512, rows - 512)]
    n = len(chunks)
    terms = 12 * RANK
    in_vmem = pl.BlockSpec(memory_space=pltpu.VMEM)
    in_hbm = pl.BlockSpec(memory_space=pltpu.HBM)
    kept = pl.pallas_call(
        functools.partial(kernel, count, chunks, factor),
        out_shape=(
            *[jax.ShapeDtypeStruct((rows // PIECES, slab), F32)] * PIECES,
            *[jax.ShapeDtypeStruct((rows // PIECES, terms), BF16)] * PIECES,
            jax.ShapeDtypeStruct((2 * RANK, slab), F32),
            jax.ShapeDtypeStruct((RANK, slab), F32),
        ),
        in_specs=[in_hbm] * 4,
        out_specs=(in_vmem,) * (2 * PIECES + 2),
        scratch_shapes=[
            pltpu.VMEM((rows, slab), F32),
            pltpu.VMEM((tokens, rows), BF16),
            pltpu.VMEM((tokens, slab), BF16),
            pltpu.VMEM((2, RANK, slab), F32),
            pltpu.VMEM((3, rows, slab), BF16),
            pltpu.VMEM((2, RANK, rows), F32),
            pltpu.VMEM((2, RANK, rows), F32),
            pltpu.VMEM((2, X, RANK, 128), F32),
            pltpu.VMEM((2 * X * C, RANK, 128), F32),
            pltpu.VMEM((Y * X * C, RANK, 128), F32),
            pltpu.SemaphoreType.DMA((3 + 2 * n,)),
            pltpu.SemaphoreType.DMA((2 * n,)),
            pltpu.SemaphoreType.DMA((2 * n,)),
            pltpu.SemaphoreType.DMA((2,)),
            pltpu.SemaphoreType.DMA((2,)),
            pltpu.SemaphoreType.REGULAR((2,)),
        ],
        compiler_params=pltpu.CompilerParams(
            collective_id=0, has_side_effects=True, vmem_limit_bytes=53480 * 1024
        ),
    )(weights[0], hidden, grad_out, warm_start)
    new_weights, next_start = pl.pallas_call(
        finish,
        out_shape=(
            jax.ShapeDtypeStruct((rows, slab), F32),
            jax.ShapeDtypeStruct((RANK, slab), F32),
        ),
        in_specs=[in_vmem] * (2 * PIECES + 2),
        out_specs=(in_hbm,) * 2,
        scratch_shapes=[
            pltpu.VMEM((rows, slab), F32),
            pltpu.SemaphoreType.DMA((PIECES + 1,)),
        ],
        compiler_params=pltpu.CompilerParams(vmem_limit_bytes=53480 * 1024),
    )(*kept)
    return new_weights[None], next_start[None]


def solution(mesh):
    return jax.shard_map(
        functools.partial(local, mesh.shape["blk"]),
        mesh=mesh,
        in_specs=(P("blk", "tp", None), P("blk", "tp"), P("blk", None), P()),
        out_specs=(P("blk", "tp", None), P("blk", None, None)),
        check_vma=False,
    )
```

```python
import functools
import math

import jax
import jax.numpy as jnp
from jax import lax
from jax.experimental import pallas as pl
from jax.experimental.pallas import tpu as pltpu
from jax.sharding import PartitionSpec as P

step_rate = 0.5
mix_rate = 0.5
MESH = pl.DeviceIdType.MESH
X, Y, C = 4, 4, 2
RANK = 8
PIECES = 14
F32, BF16 = jnp.float32, jnp.bfloat16


def split3(v):
    high = v.astype(BF16)
    rest = v - high.astype(F32)
    mid = rest.astype(BF16)
    low = (rest - mid.astype(F32)).astype(BF16)
    return high, mid, low


def dot(a, b, dims):
    return lax.dot_general(a, b, (dims, ((), ())), preferred_element_type=F32)


def folded(v):
    n = v.shape[0] // 3
    return v[:n] + (v[n : 2 * n] + v[2 * n :])


def send(src, dst, send_sem, recv_sem, peer):
    copy = pltpu.make_async_remote_copy(
        src_ref=src, dst_ref=dst, send_sem=send_sem, recv_sem=recv_sem,
        device_id=peer, device_id_type=MESH,
    )
    copy.start()
    return copy


def kernel(
    count, chunks, factor,
    w_hbm, h_hbm, g_hbm, s_hbm, *rest,
):
    steps, images, rest = rest[:PIECES], rest[PIECES : 2 * PIECES], rest[2 * PIECES :]
    mix_ref, next_ref, w_v, h_v, g_v, start_v, parts_v, own, land, part = rest[:10]
    first, second, load_sems, isend, irecv, sends, recvs, ready = rest[10:]
    tall_rows = steps[0].shape[0]
    r = lax.axis_index("blk")
    t = lax.axis_index("tp")
    core = lax.rem(t, C)
    x = lax.rem(lax.div(t, C), X)
    y = lax.div(t, C * X)
    right = lax.rem(r + 1, count)
    left = lax.rem(r + count - 1, count)
    chip = t - core
    slab = w_v.shape[1]

    def at(yy, xx, cc):
        return (yy * X + xx) * C + cc

    loads = [
        pltpu.make_async_copy(s_hbm.at[r], start_v.at[0], load_sems.at[1]),
        pltpu.make_async_copy(s_hbm.at[left], start_v.at[1], load_sems.at[2]),
    ]
    for copy in loads:
        copy.start()
    g_load = pltpu.make_async_copy(g_hbm, g_v, load_sems.at[0])
    chunk_loads = []
    for i, (lo, size) in enumerate(chunks):
        w_copy = pltpu.make_async_copy(
            w_hbm.at[pl.ds(lo, size)], w_v.at[pl.ds(lo, size)], load_sems.at[4 + 2 * i]
        )
        h_copy = pltpu.make_async_copy(
            h_hbm.at[:, pl.ds(lo, size)], h_v.at[:, pl.ds(lo, size)], load_sems.at[3 + 2 * i]
        )
        w_copy.start()
        chunk_loads.append((w_copy, h_copy))
    g_load.start()
    for pair in chunk_loads:
        pair[1].start()

    barrier = pltpu.get_barrier_semaphore()
    def turned(v, k, size):
        return lax.rem(v + k, size)

    sibling = (r, chip + 1 - core)
    x_row = [(r, at(y, turned(x, k, X), core)) for k in range(1, X)]
    y_column = [(r, at(turned(y, k, Y), x, core)) for k in range(1, Y)]
    entry = [(side, chip + cc) for side in (right, left) for cc in range(C)] + [sibling] + x_row + y_column
    around = [(ky, kx, kc) for ky in range(Y) for kx in range(X) for kc in range(C)][1:]
    around.sort(key=lambda k: -min(k[0], Y - k[0]) - min(k[1], X - k[1]))
    along_x = sorted(range(X), key=lambda k: -min(k, X - k))

    def greet(some, sem):
        for peer in some:
            pl.semaphore_signal(sem, inc=1, device_id=peer, device_id_type=MESH)

    greet(entry, barrier)

    part[...] = jnp.zeros_like(part)
    for copy in loads:
        copy.wait()
    starts = start_v[...].reshape(2 * RANK, slab)
    start_parts = split3(starts)
    tall = jnp.concatenate(start_parts, axis=0)
    n = 2 * RANK
    tall_t = tall.T

    seen = []
    for i, (lo, size) in enumerate(chunks):
        chunk_loads[i][0].wait()
        high, mid, low = [dot(v, tall_t, ((1,), (0,))) for v in split3(w_v[pl.ds(lo, size), :])]
        seen.append(folded((high + (mid + low)).T))
    g_load.wait()
    felt = factor * folded(dot(g_v[...], tall_t, ((1,), (0,))).T)
    felt_tall = jnp.concatenate(split3(felt), axis=0)
    image_copies = []
    for i, (lo, size) in enumerate(chunks):
        span = pl.ds(lo, size)
        chunk_loads[i][1].wait()
        image = seen[i] - folded(dot(felt_tall, h_v[:, span], ((1,), (0,))))
        own[0, :, span] = image[:RANK]
        own[1, :, span] = image[RANK:]
        if i == 0:
            pl.semaphore_wait(barrier, len(entry))
            greet(x_row, ready.at[0])
        image_copies.append(
            (
                send(own.at[0, :, span], land.at[1, :, span], isend.at[2 * i], irecv.at[2 * i], (right, t)),
                send(own.at[1, :, span], land.at[0, :, span], isend.at[2 * i + 1], irecv.at[2 * i + 1], (left, t)),
            )
        )

    for lo, size in chunks:
        span = pl.ds(lo, size)
        gradient = dot(h_v[:, span], g_v[...], ((0,), (0,)))
        stepped = w_v[span, :] - factor * gradient
        for p in range(lo // tall_rows, (lo + size) // tall_rows):
            steps[p][...] = stepped[p * tall_rows - lo : (p + 1) * tall_rows - lo]
        stacks = split3(stepped)
        for k in range(3):
            parts_v[k, span, :] = stacks[k]

    images_f = [[], []]
    for e in range(2):
        product = jnp.zeros((3 * RANK, slab), F32)
        gram = jnp.zeros((3 * RANK, RANK), F32)
        for i, (lo, size) in enumerate(chunks):
            span = pl.ds(lo, size)
            image_copies[i][1 - e].wait_recv()
            image = own[0, :, span] - land[0, :, span] if e == 0 else land[1, :, span] - own[1, :, span]
            images_f[e].append(image)
            pieces = split3(image)
            rows = jnp.concatenate([v.astype(F32) for v in pieces], axis=0).astype(BF16)
            for k in range(3):
                product = product + dot(rows, parts_v[k, span, :], ((1,), (0,)))
                gram = gram + dot(rows, pieces[k], ((1,), (1,)))
        product, gram = folded(product), folded(gram)
        for k in range(X - 1):
            block = product[:, 128 * k : 128 * (k + 1)]
            part[e, k] = block if e == 0 else -block
        part[e, X - 1, :, :RANK] = 0.5 * gram
        aside = lax.rem(core + e, C)
        side, taker = ((right, 1), (left, 0))[e]
        if e == 0:
            pl.semaphore_wait(ready.at[0], len(x_row))
            greet([sibling], ready.at[1])

        def across():
            for kx in along_x:
                tile = turned(x, kx, X)
                send(
                    part.at[e, tile], first.at[X * C + C * ((-kx) % X) + core], sends.at[0], recvs.at[0],
                    (side, at(y, tile, taker)),
                )

        def within():
            for kx in along_x:
                tile = turned(x, kx, X)

                def near():
                    send(
                        part.at[e, tile], first.at[C * ((-kx) % X) + aside], sends.at[0], recvs.at[0],
                        (r, at(y, tile, e)),
                    )

                if kx:
                    near()
                else:
                    pl.when(core != e)(near)

        for step in (across, within) if e == 0 else (within, across):
            step()
    first[0] = part[core, x]
    def whole(buf, step):
        return pltpu.make_async_remote_copy(
            src_ref=buf, dst_ref=buf, send_sem=sends.at[step], recv_sem=recvs.at[step],
            device_id=(r, chip + 1 - core), device_id_type=MESH,
        )

    early = first.at[pl.ds(1, first.shape[0] - 1)]
    late = second.at[pl.ds(1, second.shape[0] - 1)]
    whole(early, 0).wait_recv()
    terms = [first[k] for k in range(first.shape[0])]
    while len(terms) > 1:
        terms = [a + b for a, b in zip(terms[::2], terms[1::2])]
    second[0] = terms[0]
    pl.semaphore_wait(ready.at[1], 1)
    for ky, kx, kc in around:
        send(
            second.at[0], second.at[(((-ky) % Y) * X + (-kx) % X) * C + kc], sends.at[1], recvs.at[1],
            (r, at(turned(y, ky, Y), turned(x, kx, X), turned(core, kc, C))),
        )
    for i, (lo, size) in enumerate(chunks):
        high, mid, low = split3(jnp.concatenate([images_f[0][i], images_f[1][i]], axis=0))
        stack = jnp.concatenate([high, high, high, mid, mid, low], axis=0)
        columns = stack.T
        for p in range(lo // tall_rows, (lo + size) // tall_rows):
            images[p][...] = columns[p * tall_rows - lo : (p + 1) * tall_rows - lo]
    whole(late, 1).wait_recv()

    def total(e, tile):
        kx = lax.rem(tile - x + X, X)
        kc = lax.rem(e + core, C)
        own = [second[(lax.rem(k - y + Y, Y) * X + kx) * C + kc] for k in range(Y)]
        return (own[0] + own[1]) + (own[2] + own[3])

    place = lax.broadcasted_iota(jnp.int32, (RANK, 128), 0)
    gram = [total(e, X - 1) for e in range(2)]
    right_side = [[total(e, k) for k in range(X - 1)] for e in range(2)]
    columns = [[jnp.broadcast_to(a[:, j : j + 1], (RANK, 128)) for j in range(RANK)] for a in gram]

    def spread(v, j):
        return jnp.broadcast_to(v[j : j + 1, :], (RANK, 128))

    ends = [jnp.ones((RANK, 128), F32)] * 2
    for j in range(RANK):
        for e in range(2):
            pivot = spread(columns[e][j], j)
            scale = jnp.where(place == j, 0.0, columns[e][j] * (1.0 / pivot))
            if e == 0:
                root = 1.0 / jnp.sqrt(pivot[:1])
                for k, v in enumerate(right_side[e]):
                    next_ref[j : j + 1, 128 * k : 128 * (k + 1)] = v[j : j + 1, :] * root
            for k in range(j + 1, RANK):
                columns[e][k] = columns[e][k] - scale * spread(columns[e][k], j)
            right_side[e] = [v - scale * spread(v, j) for v in right_side[e]]
            ends[e] = jnp.where(place == j, pivot, ends[e])
    for e, sign in enumerate((mix_rate, -mix_rate)):
        inverse = sign / ends[e]
        for k, v in enumerate(right_side[e]):
            mix_ref[RANK * e : RANK * (e + 1), 128 * k : 128 * (k + 1)] = v * inverse
    for pair in image_copies:
        for copy in pair:
            copy.wait_send()
    whole(early, 0).wait_send()
    whole(late, 1).wait_send()


def finish(*refs):
    steps, images = refs[:PIECES], refs[PIECES : 2 * PIECES]
    mix_v, next_v, out_hbm, next_hbm, out_v, sems = refs[2 * PIECES :]
    tall = steps[0].shape[0]
    last = pltpu.make_async_copy(next_v, next_hbm, sems.at[PIECES])
    last.start()
    high, mid, low = split3(mix_v[...])
    mix_stack = jnp.concatenate([high, mid, low, high, mid, high], axis=0)
    stores = [last]
    for p in range(PIECES):
        span = pl.ds(p * tall, tall)
        out_v[span, :] = steps[p][...] - dot(images[p][...], mix_stack, ((1,), (0,)))
        store = pltpu.make_async_copy(out_v.at[span], out_hbm.at[span], sems.at[p])
        store.start()
        stores.append(store)
    for store in stores:
        store.wait()


def local(count, weights, hidden, grad_out, warm_start):
    _, rows, slab = weights.shape
    tokens = hidden.shape[0]
    factor = step_rate / math.sqrt(tokens)
    chunks = [(0, 512), (512, rows - 512)]
    n = len(chunks)
    terms = 12 * RANK
    in_vmem = pl.BlockSpec(memory_space=pltpu.VMEM)
    in_hbm = pl.BlockSpec(memory_space=pltpu.HBM)
    kept = pl.pallas_call(
        functools.partial(kernel, count, chunks, factor),
        out_shape=(
            *[jax.ShapeDtypeStruct((rows // PIECES, slab), F32)] * PIECES,
            *[jax.ShapeDtypeStruct((rows // PIECES, terms), BF16)] * PIECES,
            jax.ShapeDtypeStruct((2 * RANK, slab), F32),
            jax.ShapeDtypeStruct((RANK, slab), F32),
        ),
        in_specs=[in_hbm] * 4,
        out_specs=(in_vmem,) * (2 * PIECES + 2),
        scratch_shapes=[
            pltpu.VMEM((rows, slab), F32),
            pltpu.VMEM((tokens, rows), BF16),
            pltpu.VMEM((tokens, slab), BF16),
            pltpu.VMEM((2, RANK, slab), F32),
            pltpu.VMEM((3, rows, slab), BF16),
            pltpu.VMEM((2, RANK, rows), F32),
            pltpu.VMEM((2, RANK, rows), F32),
            pltpu.VMEM((2, X, RANK, 128), F32),
            pltpu.VMEM((2 * X * C, RANK, 128), F32),
            pltpu.VMEM((Y * X * C, RANK, 128), F32),
            pltpu.SemaphoreType.DMA((3 + 2 * n,)),
            pltpu.SemaphoreType.DMA((2 * n,)),
            pltpu.SemaphoreType.DMA((2 * n,)),
            pltpu.SemaphoreType.DMA((2,)),
            pltpu.SemaphoreType.DMA((2,)),
            pltpu.SemaphoreType.REGULAR((2,)),
        ],
        compiler_params=pltpu.CompilerParams(
            collective_id=0, has_side_effects=True, vmem_limit_bytes=53480 * 1024
        ),
    )(weights[0], hidden, grad_out, warm_start)
    new_weights, next_start = pl.pallas_call(
        finish,
        out_shape=(
            jax.ShapeDtypeStruct((rows, slab), F32),
            jax.ShapeDtypeStruct((RANK, slab), F32),
        ),
        in_specs=[in_vmem] * (2 * PIECES + 2),
        out_specs=(in_hbm,) * 2,
        scratch_shapes=[
            pltpu.VMEM((rows, slab), F32),
            pltpu.SemaphoreType.DMA((PIECES + 1,)),
        ],
        compiler_params=pltpu.CompilerParams(vmem_limit_bytes=53480 * 1024),
    )(*kept)
    return new_weights[None], next_start[None]


def solution(mesh):
    return jax.shard_map(
        functools.partial(local, mesh.shape["blk"]),
        mesh=mesh,
        in_specs=(P("blk", "tp", None), P("blk", "tp"), P("blk", None), P()),
        out_specs=(P("blk", "tp", None), P("blk", None, None)),
        check_vma=False,
    )
```

```python
import functools
import math

import jax
import jax.numpy as jnp
from jax import lax
from jax.experimental import pallas as pl
from jax.experimental.pallas import tpu as pltpu
from jax.sharding import PartitionSpec as P

step_rate = 0.5
mix_rate = 0.5
MESH = pl.DeviceIdType.MESH
X, Y, C = 4, 4, 2
RANK = 8
PIECES = 14
F32, BF16 = jnp.float32, jnp.bfloat16


def split3(v):
    high = v.astype(BF16)
    rest = v - high.astype(F32)
    mid = rest.astype(BF16)
    low = (rest - mid.astype(F32)).astype(BF16)
    return high, mid, low


def dot(a, b, dims):
    return lax.dot_general(a, b, (dims, ((), ())), preferred_element_type=F32)


def folded(v):
    n = v.shape[0] // 3
    return v[:n] + (v[n : 2 * n] + v[2 * n :])


def send(src, dst, send_sem, recv_sem, peer):
    copy = pltpu.make_async_remote_copy(
        src_ref=src, dst_ref=dst, send_sem=send_sem, recv_sem=recv_sem,
        device_id=peer, device_id_type=MESH,
    )
    copy.start()
    return copy


def kernel(
    count, chunks, factor,
    w_hbm, h_hbm, g_hbm, s_hbm, *rest,
):
    steps, images, rest = rest[:PIECES], rest[PIECES : 2 * PIECES], rest[2 * PIECES :]
    mix_ref, next_ref, w_v, h_v, g_v, start_v, parts_v, own, land, part = rest[:10]
    first, second, load_sems, isend, irecv, sends, recvs, ready = rest[10:]
    tall_rows = steps[0].shape[0]
    r = lax.axis_index("blk")
    t = lax.axis_index("tp")
    core = lax.rem(t, C)
    x = lax.rem(lax.div(t, C), X)
    y = lax.div(t, C * X)
    right = lax.rem(r + 1, count)
    left = lax.rem(r + count - 1, count)
    chip = t - core
    slab = w_v.shape[1]

    def at(yy, xx, cc):
        return (yy * X + xx) * C + cc

    barrier = pltpu.get_barrier_semaphore()
    def turned(v, k, size):
        return lax.rem(v + k, size)

    sibling = (r, chip + 1 - core)
    x_row = [(r, at(y, turned(x, k, X), core)) for k in range(1, X)]
    y_column = [(r, at(turned(y, k, Y), x, core)) for k in range(1, Y)]
    entry = [(side, chip + cc) for side in (right, left) for cc in range(C)] + [sibling] + x_row + y_column
    around = [(ky, kx, kc) for ky in range(Y) for kx in range(X) for kc in range(C)][1:]
    around.sort(key=lambda k: -min(k[0], Y - k[0]) - min(k[1], X - k[1]))
    along_x = sorted(range(X), key=lambda k: -min(k, X - k))

    def greet(some, sem):
        for peer in some:
            pl.semaphore_signal(sem, inc=1, device_id=peer, device_id_type=MESH)

    greet(entry[: 2 * C], barrier)
    loads = [
        pltpu.make_async_copy(s_hbm.at[r], start_v.at[0], load_sems.at[1]),
        pltpu.make_async_copy(s_hbm.at[left], start_v.at[1], load_sems.at[2]),
    ]
    for copy in loads:
        copy.start()
    g_load = pltpu.make_async_copy(g_hbm, g_v, load_sems.at[0])
    chunk_loads = []
    for i, (lo, size) in enumerate(chunks):
        w_copy = pltpu.make_async_copy(
            w_hbm.at[pl.ds(lo, size)], w_v.at[pl.ds(lo, size)], load_sems.at[4 + 2 * i]
        )
        h_copy = pltpu.make_async_copy(
            h_hbm.at[:, pl.ds(lo, size)], h_v.at[:, pl.ds(lo, size)], load_sems.at[3 + 2 * i]
        )
        w_copy.start()
        chunk_loads.append((w_copy, h_copy))
    g_load.start()
    for pair in chunk_loads:
        pair[1].start()

    greet(entry[2 * C :], barrier)

    part[...] = jnp.zeros_like(part)
    for copy in loads:
        copy.wait()
    starts = start_v[...].reshape(2 * RANK, slab)
    start_parts = split3(starts)
    tall = jnp.concatenate(start_parts, axis=0)
    n = 2 * RANK
    tall_t = tall.T

    seen = []
    for i, (lo, size) in enumerate(chunks):
        chunk_loads[i][0].wait()
        high, mid, low = [dot(v, tall_t, ((1,), (0,))) for v in split3(w_v[pl.ds(lo, size), :])]
        seen.append(folded((high + (mid + low)).T))
    g_load.wait()
    felt = factor * folded(dot(g_v[...], tall_t, ((1,), (0,))).T)
    felt_tall = jnp.concatenate(split3(felt), axis=0)
    image_copies = []
    for i, (lo, size) in enumerate(chunks):
        span = pl.ds(lo, size)
        chunk_loads[i][1].wait()
        image = seen[i] - folded(dot(felt_tall, h_v[:, span], ((1,), (0,))))
        own[0, :, span] = image[:RANK]
        own[1, :, span] = image[RANK:]
        if i == 0:
            pl.semaphore_wait(barrier, len(entry))
        image_copies.append(
            (
                send(own.at[0, :, span], land.at[1, :, span], isend.at[2 * i], irecv.at[2 * i], (right, t)),
                send(own.at[1, :, span], land.at[0, :, span], isend.at[2 * i + 1], irecv.at[2 * i + 1], (left, t)),
            )
        )
        if i == 0:
            greet(x_row, ready.at[0])

    for lo, size in chunks:
        span = pl.ds(lo, size)
        gradient = dot(h_v[:, span], g_v[...], ((0,), (0,)))
        stepped = w_v[span, :] - factor * gradient
        for p in range(lo // tall_rows, (lo + size) // tall_rows):
            steps[p][...] = stepped[p * tall_rows - lo : (p + 1) * tall_rows - lo]
        stacks = split3(stepped)
        for k in range(3):
            parts_v[k, span, :] = stacks[k]

    images_f = [[], []]
    for e in range(2):
        product = jnp.zeros((3 * RANK, slab), F32)
        gram = jnp.zeros((3 * RANK, 3 * RANK), F32)
        for i, (lo, size) in enumerate(chunks):
            span = pl.ds(lo, size)
            image_copies[i][1 - e].wait_recv()
            image = own[0, :, span] - land[0, :, span] if e == 0 else land[1, :, span] - own[1, :, span]
            images_f[e].append(image)
            pieces = split3(image)
            rows = jnp.concatenate([v.astype(F32) for v in pieces], axis=0).astype(BF16)
            gram = gram + dot(rows, rows, ((1,), (1,)))
            for k in range(3):
                product = product + dot(rows, parts_v[k, span, :], ((1,), (0,)))
        product, gram = folded(product), folded(gram)
        for k in range(X - 1):
            block = product[:, 128 * k : 128 * (k + 1)]
            part[e, k] = block if e == 0 else -block
        gram = gram[:, :RANK] + (gram[:, RANK : 2 * RANK] + gram[:, 2 * RANK :])
        part[e, X - 1, :, :RANK] = 0.5 * gram
        aside = lax.rem(core + e, C)
        side, taker = ((right, 1), (left, 0))[e]
        if e == 0:
            pl.semaphore_wait(ready.at[0], len(x_row))
            greet([sibling], ready.at[1])

        def across():
            for kx in along_x:
                tile = turned(x, kx, X)
                send(
                    part.at[e, tile], first.at[X * C + C * ((-kx) % X) + core], sends.at[0], recvs.at[0],
                    (side, at(y, tile, taker)),
                )

        def within():
            for kx in along_x:
                tile = turned(x, kx, X)

                def near():
                    send(
                        part.at[e, tile], first.at[C * ((-kx) % X) + aside], sends.at[0], recvs.at[0],
                        (r, at(y, tile, e)),
                    )

                if kx:
                    near()
                else:
                    pl.when(core != e)(near)

        for step in (across, within) if e == 0 else (within, across):
            step()
    first[0] = part[core, x]
    def whole(buf, step):
        return pltpu.make_async_remote_copy(
            src_ref=buf, dst_ref=buf, send_sem=sends.at[step], recv_sem=recvs.at[step],
            device_id=(r, chip + 1 - core), device_id_type=MESH,
        )

    early = first.at[pl.ds(1, first.shape[0] - 1)]
    late = second.at[pl.ds(1, second.shape[0] - 1)]
    whole(early, 0).wait_recv()
    terms = [first[k] for k in range(first.shape[0])]
    while len(terms) > 1:
        terms = [a + b for a, b in zip(terms[::2], terms[1::2])]
    second[0] = terms[0]
    pl.semaphore_wait(ready.at[1], 1)
    for ky, kx, kc in around:
        send(
            second.at[0], second.at[(((-ky) % Y) * X + (-kx) % X) * C + kc], sends.at[1], recvs.at[1],
            (r, at(turned(y, ky, Y), turned(x, kx, X), turned(core, kc, C))),
        )
    for i, (lo, size) in enumerate(chunks):
        high, mid, low = split3(jnp.concatenate([images_f[0][i], images_f[1][i]], axis=0))
        stack = jnp.concatenate([high, high, high, mid, mid, low], axis=0)
        columns = stack.T
        for p in range(lo // tall_rows, (lo + size) // tall_rows):
            images[p][...] = columns[p * tall_rows - lo : (p + 1) * tall_rows - lo]
    whole(late, 1).wait_recv()

    def total(e, tile):
        kx = lax.rem(tile - x + X, X)
        kc = lax.rem(e + core, C)
        own = [second[(lax.rem(k - y + Y, Y) * X + kx) * C + kc] for k in range(Y)]
        return (own[0] + own[1]) + (own[2] + own[3])

    place = lax.broadcasted_iota(jnp.int32, (RANK, 128), 0)
    gram = [total(e, X - 1) for e in range(2)]
    right_side = [[total(e, k) for k in range(X - 1)] for e in range(2)]
    columns = [[jnp.broadcast_to(a[:, j : j + 1], (RANK, 128)) for j in range(RANK)] for a in gram]

    def spread(v, j):
        return jnp.broadcast_to(v[j : j + 1, :], (RANK, 128))

    ends = [jnp.ones((RANK, 128), F32)] * 2
    for j in range(RANK):
        for e in range(2):
            pivot = spread(columns[e][j], j)
            scale = jnp.where(place == j, 0.0, columns[e][j] * (1.0 / pivot))
            if e == 0:
                root = 1.0 / jnp.sqrt(pivot[:1])
                for k, v in enumerate(right_side[e]):
                    next_ref[j : j + 1, 128 * k : 128 * (k + 1)] = v[j : j + 1, :] * root
            for k in range(j + 1, RANK):
                columns[e][k] = columns[e][k] - scale * spread(columns[e][k], j)
            right_side[e] = [v - scale * spread(v, j) for v in right_side[e]]
            ends[e] = jnp.where(place == j, pivot, ends[e])
    for e, sign in enumerate((mix_rate, -mix_rate)):
        inverse = sign / ends[e]
        for k, v in enumerate(right_side[e]):
            mix_ref[RANK * e : RANK * (e + 1), 128 * k : 128 * (k + 1)] = v * inverse
    for pair in image_copies:
        for copy in pair:
            copy.wait_send()
    whole(early, 0).wait_send()
    whole(late, 1).wait_send()


def finish(*refs):
    steps, images = refs[:PIECES], refs[PIECES : 2 * PIECES]
    mix_v, next_v, out_hbm, next_hbm, out_v, sems = refs[2 * PIECES :]
    tall = steps[0].shape[0]
    last = pltpu.make_async_copy(next_v, next_hbm, sems.at[PIECES])
    last.start()
    high, mid, low = split3(mix_v[...])
    mix_stack = jnp.concatenate([high, mid, low, high, mid, high], axis=0)
    stores = [last]
    for p in range(PIECES):
        span = pl.ds(p * tall, tall)
        out_v[span, :] = steps[p][...] - dot(images[p][...], mix_stack, ((1,), (0,)))
        store = pltpu.make_async_copy(out_v.at[span], out_hbm.at[span], sems.at[p])
        store.start()
        stores.append(store)
    for store in stores:
        store.wait()


def local(count, weights, hidden, grad_out, warm_start):
    _, rows, slab = weights.shape
    tokens = hidden.shape[0]
    factor = step_rate / math.sqrt(tokens)
    chunks = [(0, 512), (512, rows - 512)]
    n = len(chunks)
    terms = 12 * RANK
    in_vmem = pl.BlockSpec(memory_space=pltpu.VMEM)
    in_hbm = pl.BlockSpec(memory_space=pltpu.HBM)
    kept = pl.pallas_call(
        functools.partial(kernel, count, chunks, factor),
        out_shape=(
            *[jax.ShapeDtypeStruct((rows // PIECES, slab), F32)] * PIECES,
            *[jax.ShapeDtypeStruct((rows // PIECES, terms), BF16)] * PIECES,
            jax.ShapeDtypeStruct((2 * RANK, slab), F32),
            jax.ShapeDtypeStruct((RANK, slab), F32),
        ),
        in_specs=[in_hbm] * 4,
        out_specs=(in_vmem,) * (2 * PIECES + 2),
        scratch_shapes=[
            pltpu.VMEM((rows, slab), F32),
            pltpu.VMEM((tokens, rows), BF16),
            pltpu.VMEM((tokens, slab), BF16),
            pltpu.VMEM((2, RANK, slab), F32),
            pltpu.VMEM((3, rows, slab), BF16),
            pltpu.VMEM((2, RANK, rows), F32),
            pltpu.VMEM((2, RANK, rows), F32),
            pltpu.VMEM((2, X, RANK, 128), F32),
            pltpu.VMEM((2 * X * C, RANK, 128), F32),
            pltpu.VMEM((Y * X * C, RANK, 128), F32),
            pltpu.SemaphoreType.DMA((3 + 2 * n,)),
            pltpu.SemaphoreType.DMA((2 * n,)),
            pltpu.SemaphoreType.DMA((2 * n,)),
            pltpu.SemaphoreType.DMA((2,)),
            pltpu.SemaphoreType.DMA((2,)),
            pltpu.SemaphoreType.REGULAR((2,)),
        ],
        compiler_params=pltpu.CompilerParams(
            collective_id=0, has_side_effects=True, vmem_limit_bytes=53480 * 1024
        ),
    )(weights[0], hidden, grad_out, warm_start)
    new_weights, next_start = pl.pallas_call(
        finish,
        out_shape=(
            jax.ShapeDtypeStruct((rows, slab), F32),
            jax.ShapeDtypeStruct((RANK, slab), F32),
        ),
        in_specs=[in_vmem] * (2 * PIECES + 2),
        out_specs=(in_hbm,) * 2,
        scratch_shapes=[
            pltpu.VMEM((rows, slab), F32),
            pltpu.SemaphoreType.DMA((PIECES + 1,)),
        ],
        compiler_params=pltpu.CompilerParams(vmem_limit_bytes=53480 * 1024),
    )(*kept)
    return new_weights[None], next_start[None]


def solution(mesh):
    return jax.shard_map(
        functools.partial(local, mesh.shape["blk"]),
        mesh=mesh,
        in_specs=(P("blk", "tp", None), P("blk", "tp"), P("blk", None), P()),
        out_specs=(P("blk", "tp", None), P("blk", None, None)),
        check_vma=False,
    )
```

```python
import functools
import math

import jax
import jax.numpy as jnp
from jax import lax
from jax.experimental import pallas as pl
from jax.experimental.pallas import tpu as pltpu
from jax.sharding import PartitionSpec as P

step_rate = 0.5
mix_rate = 0.5
MESH = pl.DeviceIdType.MESH
X, Y, C = 4, 4, 2
RANK = 8
PIECES = 14
F32, BF16 = jnp.float32, jnp.bfloat16


def split3(v):
    high = v.astype(BF16)
    rest = v - high.astype(F32)
    mid = rest.astype(BF16)
    low = (rest - mid.astype(F32)).astype(BF16)
    return high, mid, low


def dot(a, b, dims):
    return lax.dot_general(a, b, (dims, ((), ())), preferred_element_type=F32)


def folded(v):
    n = v.shape[0] // 3
    return v[:n] + (v[n : 2 * n] + v[2 * n :])


def send(src, dst, send_sem, recv_sem, peer):
    copy = pltpu.make_async_remote_copy(
        src_ref=src, dst_ref=dst, send_sem=send_sem, recv_sem=recv_sem,
        device_id=peer, device_id_type=MESH,
    )
    copy.start()
    return copy


def kernel(
    count, chunks, factor,
    w_hbm, h_hbm, g_hbm, s_hbm, *rest,
):
    steps, images, rest = rest[:PIECES], rest[PIECES : 2 * PIECES], rest[2 * PIECES :]
    mix_ref, next_ref, w_v, h_v, g_v, start_v, parts_v, own, land, part = rest[:10]
    first, second, load_sems, isend, irecv, sends, recvs, ready = rest[10:]
    tall_rows = steps[0].shape[0]
    r = lax.axis_index("blk")
    t = lax.axis_index("tp")
    core = lax.rem(t, C)
    x = lax.rem(lax.div(t, C), X)
    y = lax.div(t, C * X)
    right = lax.rem(r + 1, count)
    left = lax.rem(r + count - 1, count)
    chip = t - core
    slab = w_v.shape[1]

    def at(yy, xx, cc):
        return (yy * X + xx) * C + cc

    loads = [
        pltpu.make_async_copy(s_hbm.at[r], start_v.at[0], load_sems.at[1]),
        pltpu.make_async_copy(s_hbm.at[left], start_v.at[1], load_sems.at[2]),
    ]
    for copy in loads:
        copy.start()
    g_load = pltpu.make_async_copy(g_hbm, g_v, load_sems.at[0])
    chunk_loads = []
    for i, (lo, size) in enumerate(chunks):
        w_copy = pltpu.make_async_copy(
            w_hbm.at[pl.ds(lo, size)], w_v.at[pl.ds(lo, size)], load_sems.at[4 + 2 * i]
        )
        h_copy = pltpu.make_async_copy(
            h_hbm.at[:, pl.ds(lo, size)], h_v.at[:, pl.ds(lo, size)], load_sems.at[3 + 2 * i]
        )
        w_copy.start()
        chunk_loads.append((w_copy, h_copy))
    g_load.start()
    for pair in chunk_loads:
        pair[1].start()

    barrier = pltpu.get_barrier_semaphore()
    def turned(v, k, size):
        return lax.rem(v + k, size)

    sibling = (r, chip + 1 - core)
    x_row = [(r, at(y, turned(x, k, X), core)) for k in range(1, X)]
    y_column = [(r, at(turned(y, k, Y), x, core)) for k in range(1, Y)]
    entry = [(side, chip + cc) for side in (right, left) for cc in range(C)] + [sibling] + x_row + y_column
    around = [(ky, kx, kc) for ky in range(Y) for kx in range(X) for kc in range(C)][1:]
    around.sort(key=lambda k: -min(k[0], Y - k[0]) - min(k[1], X - k[1]))
    along_x = sorted(range(X), key=lambda k: -min(k, X - k))

    def greet(some, sem):
        for peer in some:
            pl.semaphore_signal(sem, inc=1, device_id=peer, device_id_type=MESH)

    greet(entry, barrier)

    part[...] = jnp.zeros_like(part)
    for copy in loads:
        copy.wait()
    starts = start_v[...].reshape(2 * RANK, slab)
    start_parts = split3(starts)
    tall = jnp.concatenate(start_parts, axis=0)
    n = 2 * RANK
    tall_t = tall.T

    seen = []
    for i, (lo, size) in enumerate(chunks):
        chunk_loads[i][0].wait()
        high, mid, low = [dot(v, tall_t, ((1,), (0,))) for v in split3(w_v[pl.ds(lo, size), :])]
        seen.append(folded((high + (mid + low)).T))
    g_load.wait()
    felt = factor * folded(dot(g_v[...], tall_t, ((1,), (0,))).T)
    felt_tall = jnp.concatenate(split3(felt), axis=0)
    image_copies = []
    for i, (lo, size) in enumerate(chunks):
        span = pl.ds(lo, size)
        chunk_loads[i][1].wait()
        image = seen[i] - folded(dot(felt_tall, h_v[:, span], ((1,), (0,))))
        own[0, :, span] = image[:RANK]
        own[1, :, span] = image[RANK:]
        if i == 0:
            pl.semaphore_wait(barrier, len(entry))
            greet(x_row, ready.at[0])
        image_copies.append(
            (
                send(own.at[0, :, span], land.at[1, :, span], isend.at[2 * i], irecv.at[2 * i], (right, t)),
                send(own.at[1, :, span], land.at[0, :, span], isend.at[2 * i + 1], irecv.at[2 * i + 1], (left, t)),
            )
        )

    for lo, size in chunks:
        span = pl.ds(lo, size)
        gradient = dot(h_v[:, span], g_v[...], ((0,), (0,)))
        stepped = w_v[span, :] - factor * gradient
        for p in range(lo // tall_rows, (lo + size) // tall_rows):
            steps[p][...] = stepped[p * tall_rows - lo : (p + 1) * tall_rows - lo]
        stacks = split3(stepped)
        for k in range(3):
            parts_v[k, span, :] = stacks[k]

    images_f = [[], []]
    for e in range(2):
        product = jnp.zeros((3 * RANK, slab), F32)
        gram = jnp.zeros((3 * RANK, RANK), F32)
        for i, (lo, size) in enumerate(chunks):
            span = pl.ds(lo, size)
            image_copies[i][1 - e].wait_recv()
            image = own[0, :, span] - land[0, :, span] if e == 0 else land[1, :, span] - own[1, :, span]
            images_f[e].append(image)
            pieces = split3(image)
            rows = jnp.concatenate([v.astype(F32) for v in pieces], axis=0).astype(BF16)
            for k in range(3):
                product = product + dot(rows, parts_v[k, span, :], ((1,), (0,)))
                gram = gram + dot(rows, pieces[k], ((1,), (1,)))
        product, gram = folded(product), folded(gram)
        for k in range(X - 1):
            block = product[:, 128 * k : 128 * (k + 1)]
            part[e, k] = block if e == 0 else -block
        part[e, X - 1, :, :RANK] = 0.5 * gram
        aside = lax.rem(core + e, C)
        side, taker = ((right, 1), (left, 0))[e]
        if e == 0:
            pl.semaphore_wait(ready.at[0], len(x_row))
            greet([sibling], ready.at[1])

        def across():
            for kx in along_x:
                tile = turned(x, kx, X)
                send(
                    part.at[e, tile], first.at[X * C + C * ((-kx) % X) + core], sends.at[0], recvs.at[0],
                    (side, at(y, tile, taker)),
                )

        def within():
            for kx in along_x:
                tile = turned(x, kx, X)

                def near():
                    send(
                        part.at[e, tile], first.at[C * ((-kx) % X) + aside], sends.at[0], recvs.at[0],
                        (r, at(y, tile, e)),
                    )

                if kx:
                    near()
                else:
                    pl.when(core != e)(near)

        for step in (across, within) if e == 0 else (within, across):
            step()
    first[0] = part[core, x]
    def whole(buf, step):
        return pltpu.make_async_remote_copy(
            src_ref=buf, dst_ref=buf, send_sem=sends.at[step], recv_sem=recvs.at[step],
            device_id=(r, chip + 1 - core), device_id_type=MESH,
        )

    early = first.at[pl.ds(1, first.shape[0] - 1)]
    late = second.at[pl.ds(1, second.shape[0] - 1)]
    whole(early, 0).wait_recv()
    terms = [first[k] for k in range(first.shape[0])]
    while len(terms) > 1:
        terms = [a + b for a, b in zip(terms[::2], terms[1::2])]
    second[0] = terms[0]
    pl.semaphore_wait(ready.at[1], 1)
    for ky, kx, kc in around:
        send(
            second.at[0], second.at[(((-ky) % Y) * X + (-kx) % X) * C + kc], sends.at[1], recvs.at[1],
            (r, at(turned(y, ky, Y), turned(x, kx, X), turned(core, kc, C))),
        )
    for i, (lo, size) in enumerate(chunks):
        high, mid, low = split3(jnp.concatenate([images_f[0][i], images_f[1][i]], axis=0))
        stack = jnp.concatenate([high, high, high, mid, mid, low], axis=0)
        columns = stack.T
        for p in range(lo // tall_rows, (lo + size) // tall_rows):
            images[p][...] = columns[p * tall_rows - lo : (p + 1) * tall_rows - lo]
    whole(late, 1).wait_recv()

    def total(e, tile):
        kx = lax.rem(tile - x + X, X)
        kc = lax.rem(e + core, C)
        own = [second[(lax.rem(k - y + Y, Y) * X + kx) * C + kc] for k in range(Y)]
        return (own[0] + own[1]) + (own[2] + own[3])

    place = lax.broadcasted_iota(jnp.int32, (RANK, 128), 0)
    gram = [total(e, X - 1) for e in range(2)]
    right_side = [[total(e, k) for k in range(X - 1)] for e in range(2)]
    columns = [[jnp.broadcast_to(a[:, j : j + 1], (RANK, 128)) for j in range(RANK)] for a in gram]

    def spread(v, j):
        return jnp.broadcast_to(v[j : j + 1, :], (RANK, 128))

    ends = [jnp.ones((RANK, 128), F32)] * 2
    for j in range(RANK):
        for e in range(2):
            pivot = spread(columns[e][j], j)
            scale = jnp.where(place == j, 0.0, columns[e][j] * (1.0 / pivot))
            if e == 0:
                root = 1.0 / jnp.sqrt(pivot[:1])
                for k, v in enumerate(right_side[e]):
                    next_ref[j : j + 1, 128 * k : 128 * (k + 1)] = v[j : j + 1, :] * root
            for k in range(j + 1, RANK):
                columns[e][k] = columns[e][k] - scale * spread(columns[e][k], j)
            right_side[e] = [v - scale * spread(v, j) for v in right_side[e]]
            ends[e] = jnp.where(place == j, pivot, ends[e])
    for e, sign in enumerate((mix_rate, -mix_rate)):
        inverse = sign / ends[e]
        for k, v in enumerate(right_side[e]):
            mix_ref[RANK * e : RANK * (e + 1), 128 * k : 128 * (k + 1)] = v * inverse
    for pair in image_copies:
        for copy in pair:
            copy.wait_send()
    whole(early, 0).wait_send()
    whole(late, 1).wait_send()


def finish(*refs):
    steps, images = refs[:PIECES], refs[PIECES : 2 * PIECES]
    mix_v, next_v, out_hbm, next_hbm, out_v, sems = refs[2 * PIECES :]
    tall = steps[0].shape[0]
    last = pltpu.make_async_copy(next_v, next_hbm, sems.at[PIECES])
    last.start()
    high, mid, low = split3(mix_v[...])
    mix_stack = jnp.concatenate([high, mid, low, high, mid, high], axis=0)
    stores = [last]
    for p in range(PIECES):
        span = pl.ds(p * tall, tall)
        out_v[span, :] = steps[p][...] - dot(images[p][...], mix_stack, ((1,), (0,)))
        store = pltpu.make_async_copy(out_v.at[span], out_hbm.at[span], sems.at[p])
        store.start()
        stores.append(store)
    for store in stores:
        store.wait()


def local(count, weights, hidden, grad_out, warm_start):
    _, rows, slab = weights.shape
    tokens = hidden.shape[0]
    factor = step_rate / math.sqrt(tokens)
    chunks = [(0, 640), (640, rows - 640)]
    n = len(chunks)
    terms = 12 * RANK
    in_vmem = pl.BlockSpec(memory_space=pltpu.VMEM)
    in_hbm = pl.BlockSpec(memory_space=pltpu.HBM)
    kept = pl.pallas_call(
        functools.partial(kernel, count, chunks, factor),
        out_shape=(
            *[jax.ShapeDtypeStruct((rows // PIECES, slab), F32)] * PIECES,
            *[jax.ShapeDtypeStruct((rows // PIECES, terms), BF16)] * PIECES,
            jax.ShapeDtypeStruct((2 * RANK, slab), F32),
            jax.ShapeDtypeStruct((RANK, slab), F32),
        ),
        in_specs=[in_hbm] * 4,
        out_specs=(in_vmem,) * (2 * PIECES + 2),
        scratch_shapes=[
            pltpu.VMEM((rows, slab), F32),
            pltpu.VMEM((tokens, rows), BF16),
            pltpu.VMEM((tokens, slab), BF16),
            pltpu.VMEM((2, RANK, slab), F32),
            pltpu.VMEM((3, rows, slab), BF16),
            pltpu.VMEM((2, RANK, rows), F32),
            pltpu.VMEM((2, RANK, rows), F32),
            pltpu.VMEM((2, X, RANK, 128), F32),
            pltpu.VMEM((2 * X * C, RANK, 128), F32),
            pltpu.VMEM((Y * X * C, RANK, 128), F32),
            pltpu.SemaphoreType.DMA((3 + 2 * n,)),
            pltpu.SemaphoreType.DMA((2 * n,)),
            pltpu.SemaphoreType.DMA((2 * n,)),
            pltpu.SemaphoreType.DMA((2,)),
            pltpu.SemaphoreType.DMA((2,)),
            pltpu.SemaphoreType.REGULAR((2,)),
        ],
        compiler_params=pltpu.CompilerParams(
            collective_id=0, has_side_effects=True, vmem_limit_bytes=53480 * 1024
        ),
    )(weights[0], hidden, grad_out, warm_start)
    new_weights, next_start = pl.pallas_call(
        finish,
        out_shape=(
            jax.ShapeDtypeStruct((rows, slab), F32),
            jax.ShapeDtypeStruct((RANK, slab), F32),
        ),
        in_specs=[in_vmem] * (2 * PIECES + 2),
        out_specs=(in_hbm,) * 2,
        scratch_shapes=[
            pltpu.VMEM((rows, slab), F32),
            pltpu.SemaphoreType.DMA((PIECES + 1,)),
        ],
        compiler_params=pltpu.CompilerParams(vmem_limit_bytes=53480 * 1024),
    )(*kept)
    return new_weights[None], next_start[None]


def solution(mesh):
    return jax.shard_map(
        functools.partial(local, mesh.shape["blk"]),
        mesh=mesh,
        in_specs=(P("blk", "tp", None), P("blk", "tp"), P("blk", None), P()),
        out_specs=(P("blk", "tp", None), P("blk", None, None)),
        check_vma=False,
    )
```

```python
import functools
import math

import jax
import jax.numpy as jnp
from jax import lax
from jax.experimental import pallas as pl
from jax.experimental.pallas import tpu as pltpu
from jax.sharding import PartitionSpec as P

step_rate = 0.5
mix_rate = 0.5
MESH = pl.DeviceIdType.MESH
X, Y, C = 4, 4, 2
RANK = 8
PIECES = 14
F32, BF16 = jnp.float32, jnp.bfloat16


def split3(v):
    high = v.astype(BF16)
    rest = v - high.astype(F32)
    mid = rest.astype(BF16)
    low = (rest - mid.astype(F32)).astype(BF16)
    return high, mid, low


def dot(a, b, dims):
    return lax.dot_general(a, b, (dims, ((), ())), preferred_element_type=F32)


def folded(v):
    n = v.shape[0] // 3
    return v[:n] + (v[n : 2 * n] + v[2 * n :])


def send(src, dst, send_sem, recv_sem, peer):
    copy = pltpu.make_async_remote_copy(
        src_ref=src, dst_ref=dst, send_sem=send_sem, recv_sem=recv_sem,
        device_id=peer, device_id_type=MESH,
    )
    copy.start()
    return copy


def kernel(
    count, chunks, factor,
    w_hbm, h_hbm, g_hbm, s_hbm, *rest,
):
    steps, images, rest = rest[:PIECES], rest[PIECES : 2 * PIECES], rest[2 * PIECES :]
    mix_ref, next_ref, w_v, h_v, g_v, start_v, parts_v, own, land, part = rest[:10]
    first, second, load_sems, isend, irecv, sends, recvs, ready = rest[10:]
    tall_rows = steps[0].shape[0]
    r = lax.axis_index("blk")
    t = lax.axis_index("tp")
    core = lax.rem(t, C)
    x = lax.rem(lax.div(t, C), X)
    y = lax.div(t, C * X)
    right = lax.rem(r + 1, count)
    left = lax.rem(r + count - 1, count)
    chip = t - core
    slab = w_v.shape[1]

    def at(yy, xx, cc):
        return (yy * X + xx) * C + cc

    loads = [
        pltpu.make_async_copy(s_hbm.at[r], start_v.at[0], load_sems.at[1]),
        pltpu.make_async_copy(s_hbm.at[left], start_v.at[1], load_sems.at[2]),
    ]
    for copy in loads:
        copy.start()
    g_load = pltpu.make_async_copy(g_hbm, g_v, load_sems.at[0])
    chunk_loads = []
    for i, (lo, size) in enumerate(chunks):
        w_copy = pltpu.make_async_copy(
            w_hbm.at[pl.ds(lo, size)], w_v.at[pl.ds(lo, size)], load_sems.at[4 + 2 * i]
        )
        h_copy = pltpu.make_async_copy(
            h_hbm.at[:, pl.ds(lo, size)], h_v.at[:, pl.ds(lo, size)], load_sems.at[3 + 2 * i]
        )
        w_copy.start()
        chunk_loads.append((w_copy, h_copy))
    g_load.start()
    for pair in chunk_loads:
        pair[1].start()

    barrier = pltpu.get_barrier_semaphore()
    def turned(v, k, size):
        return lax.rem(v + k, size)

    sibling = (r, chip + 1 - core)
    x_row = [(r, at(y, turned(x, k, X), core)) for k in range(1, X)]
    y_column = [(r, at(turned(y, k, Y), x, core)) for k in range(1, Y)]
    entry = [(side, chip + cc) for side in (right, left) for cc in range(C)] + [sibling] + x_row + y_column
    around = [(ky, kx, kc) for ky in range(Y) for kx in range(X) for kc in range(C)][1:]
    around.sort(key=lambda k: -min(k[0], Y - k[0]) - min(k[1], X - k[1]))
    along_x = sorted(range(X), key=lambda k: -min(k, X - k))

    def greet(some, sem):
        for peer in some:
            pl.semaphore_signal(sem, inc=1, device_id=peer, device_id_type=MESH)

    greet(entry, barrier)

    part[...] = jnp.zeros_like(part)
    for copy in loads:
        copy.wait()
    starts = start_v[...].reshape(2 * RANK, slab)
    start_parts = split3(starts)
    tall = jnp.concatenate(start_parts, axis=0)
    n = 2 * RANK
    tall_t = tall.T

    seen = []
    for i, (lo, size) in enumerate(chunks):
        chunk_loads[i][0].wait()
        high, mid, low = [dot(v, tall_t, ((1,), (0,))) for v in split3(w_v[pl.ds(lo, size), :])]
        seen.append(folded((high + (mid + low)).T))
    g_load.wait()
    felt = factor * folded(dot(g_v[...], tall_t, ((1,), (0,))).T)
    felt_tall = jnp.concatenate(split3(felt), axis=0)
    image_copies = []
    for i, (lo, size) in enumerate(chunks):
        span = pl.ds(lo, size)
        chunk_loads[i][1].wait()
        image = seen[i] - folded(dot(felt_tall, h_v[:, span], ((1,), (0,))))
        own[0, :, span] = image[:RANK]
        own[1, :, span] = image[RANK:]
        if i == 0:
            pl.semaphore_wait(barrier, len(entry))
            greet(x_row, ready.at[0])
        image_copies.append(
            (
                send(own.at[0, :, span], land.at[1, :, span], isend.at[2 * i], irecv.at[2 * i], (right, t)),
                send(own.at[1, :, span], land.at[0, :, span], isend.at[2 * i + 1], irecv.at[2 * i + 1], (left, t)),
            )
        )

    for lo, size in chunks:
        span = pl.ds(lo, size)
        gradient = dot(h_v[:, span], g_v[...], ((0,), (0,)))
        stepped = w_v[span, :] - factor * gradient
        for p in range(lo // tall_rows, (lo + size) // tall_rows):
            steps[p][...] = stepped[p * tall_rows - lo : (p + 1) * tall_rows - lo]
        stacks = split3(stepped)
        for k in range(3):
            parts_v[k, span, :] = stacks[k]

    images_f = [[], []]
    for e in range(2):
        product = jnp.zeros((3 * RANK, slab), F32)
        gram = jnp.zeros((3 * RANK, 3 * RANK), F32)
        for i, (lo, size) in enumerate(chunks):
            span = pl.ds(lo, size)
            image_copies[i][1 - e].wait_recv()
            image = own[0, :, span] - land[0, :, span] if e == 0 else land[1, :, span] - own[1, :, span]
            images_f[e].append(image)
            pieces = split3(image)
            rows = jnp.concatenate([v.astype(F32) for v in pieces], axis=0).astype(BF16)
            gram = gram + dot(rows, rows, ((1,), (1,)))
            for k in range(3):
                product = product + dot(rows, parts_v[k, span, :], ((1,), (0,)))
        product, gram = folded(product), folded(gram)
        for k in range(X - 1):
            block = product[:, 128 * k : 128 * (k + 1)]
            part[e, k] = block if e == 0 else -block
        gram = gram[:, :RANK] + (gram[:, RANK : 2 * RANK] + gram[:, 2 * RANK :])
        part[e, X - 1, :, :RANK] = 0.5 * gram
        aside = lax.rem(core + e, C)
        side, taker = ((right, 1), (left, 0))[e]
        if e == 0:
            pl.semaphore_wait(ready.at[0], len(x_row))
            greet([sibling], ready.at[1])

        def across():
            for kx in along_x:
                tile = turned(x, kx, X)
                send(
                    part.at[e, tile], first.at[X * C + C * ((-kx) % X) + core], sends.at[0], recvs.at[0],
                    (side, at(y, tile, taker)),
                )

        def within():
            for kx in along_x:
                tile = turned(x, kx, X)

                def near():
                    send(
                        part.at[e, tile], first.at[C * ((-kx) % X) + aside], sends.at[0], recvs.at[0],
                        (r, at(y, tile, e)),
                    )

                if kx:
                    near()
                else:
                    pl.when(core != e)(near)

        for step in (across, within) if e == 0 else (within, across):
            step()
    first[0] = part[core, x]
    def whole(buf, step):
        return pltpu.make_async_remote_copy(
            src_ref=buf, dst_ref=buf, send_sem=sends.at[step], recv_sem=recvs.at[step],
            device_id=(r, chip + 1 - core), device_id_type=MESH,
        )

    early = first.at[pl.ds(1, first.shape[0] - 1)]
    late = second.at[pl.ds(1, second.shape[0] - 1)]
    whole(early, 0).wait_recv()
    terms = [first[k] for k in range(first.shape[0])]
    while len(terms) > 1:
        terms = [a + b for a, b in zip(terms[::2], terms[1::2])]
    second[0] = terms[0]
    pl.semaphore_wait(ready.at[1], 1)
    for ky, kx, kc in around:
        send(
            second.at[0], second.at[(((-ky) % Y) * X + (-kx) % X) * C + kc], sends.at[1], recvs.at[1],
            (r, at(turned(y, ky, Y), turned(x, kx, X), turned(core, kc, C))),
        )
    for i, (lo, size) in enumerate(chunks):
        high, mid, low = split3(jnp.concatenate([images_f[0][i], images_f[1][i]], axis=0))
        stack = jnp.concatenate([high, high, high, mid, mid, low], axis=0)
        columns = stack.T
        for p in range(lo // tall_rows, (lo + size) // tall_rows):
            images[p][...] = columns[p * tall_rows - lo : (p + 1) * tall_rows - lo]
    whole(late, 1).wait_recv()

    def total(e, tile):
        kx = lax.rem(tile - x + X, X)
        kc = lax.rem(e + core, C)
        own = [second[(lax.rem(k - y + Y, Y) * X + kx) * C + kc] for k in range(Y)]
        return (own[0] + own[1]) + (own[2] + own[3])

    place = lax.broadcasted_iota(jnp.int32, (RANK, 128), 0)
    gram = [total(e, X - 1) for e in range(2)]
    right_side = [[total(e, k) for k in range(X - 1)] for e in range(2)]
    columns = [[jnp.broadcast_to(a[:, j : j + 1], (RANK, 128)) for j in range(RANK)] for a in gram]

    def spread(v, j):
        return jnp.broadcast_to(v[j : j + 1, :], (RANK, 128))

    ends = [jnp.ones((RANK, 128), F32)] * 2
    for j in range(RANK):
        for e in range(2):
            pivot = spread(columns[e][j], j)
            scale = jnp.where(place == j, 0.0, columns[e][j] * (1.0 / pivot))
            if e == 0:
                root = 1.0 / jnp.sqrt(pivot[:1])
                for k, v in enumerate(right_side[e]):
                    next_ref[j : j + 1, 128 * k : 128 * (k + 1)] = v[j : j + 1, :] * root
            for k in range(j + 1, RANK):
                columns[e][k] = columns[e][k] - scale * spread(columns[e][k], j)
            right_side[e] = [v - scale * spread(v, j) for v in right_side[e]]
            ends[e] = jnp.where(place == j, pivot, ends[e])
    for e, sign in enumerate((mix_rate, -mix_rate)):
        inverse = sign / ends[e]
        for k, v in enumerate(right_side[e]):
            mix_ref[RANK * e : RANK * (e + 1), 128 * k : 128 * (k + 1)] = v * inverse
    for pair in image_copies:
        for copy in pair:
            copy.wait_send()
    whole(early, 0).wait_send()
    whole(late, 1).wait_send()


def finish(*refs):
    steps, images = refs[:PIECES], refs[PIECES : 2 * PIECES]
    mix_v, next_v, out_hbm, next_hbm, out_v, sems = refs[2 * PIECES :]
    tall = steps[0].shape[0]
    last = pltpu.make_async_copy(next_v, next_hbm, sems.at[PIECES])
    last.start()
    high, mid, low = split3(mix_v[...])
    mix_stack = jnp.concatenate([high, mid, low, high, mid, high], axis=0)
    stores = [last]
    for p in range(PIECES):
        span = pl.ds(p * tall, tall)
        out_v[span, :] = steps[p][...] - dot(images[p][...], mix_stack, ((1,), (0,)))
        store = pltpu.make_async_copy(out_v.at[span], out_hbm.at[span], sems.at[p])
        store.start()
        stores.append(store)
    for store in stores:
        store.wait()


def local(count, weights, hidden, grad_out, warm_start):
    _, rows, slab = weights.shape
    tokens = hidden.shape[0]
    factor = step_rate / math.sqrt(tokens)
    chunks = [(0, 512), (512, rows - 512)]
    n = len(chunks)
    terms = 12 * RANK
    in_vmem = pl.BlockSpec(memory_space=pltpu.VMEM)
    in_hbm = pl.BlockSpec(memory_space=pltpu.HBM)
    kept = pl.pallas_call(
        functools.partial(kernel, count, chunks, factor),
        out_shape=(
            *[jax.ShapeDtypeStruct((rows // PIECES, slab), F32)] * PIECES,
            *[jax.ShapeDtypeStruct((rows // PIECES, terms), BF16)] * PIECES,
            jax.ShapeDtypeStruct((2 * RANK, slab), F32),
            jax.ShapeDtypeStruct((RANK, slab), F32),
        ),
        in_specs=[in_hbm] * 4,
        out_specs=(in_vmem,) * (2 * PIECES + 2),
        scratch_shapes=[
            pltpu.VMEM((rows, slab), F32),
            pltpu.VMEM((tokens, rows), BF16),
            pltpu.VMEM((tokens, slab), BF16),
            pltpu.VMEM((2, RANK, slab), F32),
            pltpu.VMEM((3, rows, slab), BF16),
            pltpu.VMEM((2, RANK, rows), F32),
            pltpu.VMEM((2, RANK, rows), F32),
            pltpu.VMEM((2, X, RANK, 128), F32),
            pltpu.VMEM((2 * X * C, RANK, 128), F32),
            pltpu.VMEM((Y * X * C, RANK, 128), F32),
            pltpu.SemaphoreType.DMA((3 + 2 * n,)),
            pltpu.SemaphoreType.DMA((2 * n,)),
            pltpu.SemaphoreType.DMA((2 * n,)),
            pltpu.SemaphoreType.DMA((2,)),
            pltpu.SemaphoreType.DMA((2,)),
            pltpu.SemaphoreType.REGULAR((2,)),
        ],
        compiler_params=pltpu.CompilerParams(
            collective_id=0, has_side_effects=True, vmem_limit_bytes=53480 * 1024
        ),
    )(weights[0], hidden, grad_out, warm_start)
    new_weights, next_start = pl.pallas_call(
        finish,
        out_shape=(
            jax.ShapeDtypeStruct((rows, slab), F32),
            jax.ShapeDtypeStruct((RANK, slab), F32),
        ),
        in_specs=[in_vmem] * (2 * PIECES + 2),
        out_specs=(in_hbm,) * 2,
        scratch_shapes=[
            pltpu.VMEM((rows, slab), F32),
            pltpu.SemaphoreType.DMA((PIECES + 1,)),
        ],
        compiler_params=pltpu.CompilerParams(vmem_limit_bytes=53480 * 1024),
    )(*kept)
    return new_weights[None], next_start[None]


def solution(mesh):
    return jax.shard_map(
        functools.partial(local, mesh.shape["blk"]),
        mesh=mesh,
        in_specs=(P("blk", "tp", None), P("blk", "tp"), P("blk", None), P()),
        out_specs=(P("blk", "tp", None), P("blk", None, None)),
        check_vma=False,
    )
```
